256 devices in a mesh: gz: 16 (over z_hi, x, core), gx: 16 (over y, z_lo).
Axes of the slice: x: 4, y: 4, z: 8 (z_hi: 2, z_lo: 4; z = z_hi * 4 + z_lo), core: 2. Of those that a mesh axis runs over, the one named last changes fastest.
Arguments:
- flow_pops: float32 [19, 512, 128, 128], P(None, 'gz', 'gx')
- tracer_pops: float32 [7, 512, 128, 128], P(None, 'gz', 'gx')
- pore_mask: int32 [512, 128, 128], P('gz', 'gx'), may hold values from 0 to 1, as said below
- relax_rates: float32 [19], replicated, may hold values from 0.7 to 1.8
- window_step: int32 [1], replicated, may hold values from 1 to 31
- start_slab: int32 [1], replicated, may hold values from 0 to 16383
Outputs:
- flow_out: float32 [19, 512, 128, 128], P(None, 'gz', 'gx')
- tracer_out: float32 [7, 512, 128, 128], P(None, 'gz', 'gx')
The draws below stay inside these ranges and needn't reach their ends.
Inputs may be any that keep to these rules, and one draw needn't show every extreme that they name: `pore_mask`: 1 marks pore space, 0 rock; the pore fraction may differ from one slab of 32 cells along z to the next.
All inputs are finite; a program needn't handle non-finite values.
Results may differ from the reference program's by a relative error of at most 0.0001.
Values sent between devices are 32-bit elements; how exact they have to be, the bound alone decides.
No kernel may reach another device: no remote copies, remote signals or barrier semaphores. Data moves between devices by JAX's collectives and lax.ppermute only.
A program may use at most 64 MiB of HBM per device.

```python
import jax
import jax.numpy as jnp
import numpy as np
from jax import lax

CZ = 32
NY = 128
NZ = 512
NX = 128
SLABS = 16


def velocity_table_drawn():
    return np.array([(0, 0, 0), (1, 0, 0), (-1, 0, 0), (0, 1, 0), (0, -1, 0), (0, 0, 1), (0, 0, -1), (1, 1, 0), (-1, -1, 0), (1, -1, 0), (-1, 1, 0), (1, 0, 1), (-1, 0, -1), (1, 0, -1), (-1, 0, 1), (0, 1, 1), (0, -1, -1), (0, 1, -1), (0, -1, 1)], dtype=np.float32)


def flow_weights_drawn():
    return np.array([1.0 / 3.0] + [1.0 / 18.0] * 6 + [1.0 / 36.0] * 12, dtype=np.float32)


def tracer_weights_drawn():
    return np.array([0.25] + [0.125] * 6, dtype=np.float32)


def draw_flow_pops(key, part):
    keys = jax.random.split(jax.random.fold_in(key, 11), 3)
    density = 1.0 + jax.random.uniform(keys[0], (NZ, NX, NY), jnp.float32, -0.1, 0.1)
    momentum = jax.random.uniform(keys[1], (3, NZ, NX, NY), jnp.float32, -0.08, 0.08)
    lattice = velocity_table_drawn()
    projected = lattice[:, 0][:, None, None, None] * momentum[0][None] + lattice[:, 1][:, None, None, None] * momentum[1][None] + lattice[:, 2][:, None, None, None] * momentum[2][None]
    momentum_sq = momentum[0] * momentum[0] + momentum[1] * momentum[1] + momentum[2] * momentum[2]
    weights = flow_weights_drawn()[:, None, None, None]
    equilibrium = weights * (density[None] + 3.0 * projected + 4.5 * projected * projected - 1.5 * momentum_sq[None])
    noise = jax.random.uniform(keys[2], (19, NZ, NX, NY), jnp.float32, -1.0, 1.0)
    return (equilibrium * (1.0 + 0.3 * noise)).astype(jnp.float32)


def draw_tracer_pops(key, part):
    keys = jax.random.split(jax.random.fold_in(key, 23), 2)
    concentration = jnp.exp(jax.random.uniform(keys[0], (NZ, NX, NY), jnp.float32, -1.6, 0.7))
    noise = jax.random.uniform(keys[1], (7, NZ, NX, NY), jnp.float32, -1.0, 1.0)
    weights = tracer_weights_drawn()[:, None, None, None]
    return (weights * concentration[None] * (1.0 + 0.3 * noise)).astype(jnp.float32)


def draw_pore_mask(key, part):
    keys = jax.random.split(jax.random.fold_in(key, 37), 2)
    levels = jax.random.randint(keys[0], (NZ // CZ,), 30, 91)
    level_rows = jnp.repeat(levels, CZ)
    rolled = jax.random.randint(keys[1], (NZ, NX, NY), 0, 100)
    return (rolled < level_rows[:, None, None]).astype(jnp.int32)


def setup_inputs(seed: int = 0) -> dict:
    key_of = jax.random.split(jax.random.key(seed), 7)
    return {
        "flow_pops": draw_flow_pops(jax.random.fold_in(key_of[6], 71), 0),
        "tracer_pops": draw_tracer_pops(jax.random.fold_in(key_of[6], 71), 0),
        "pore_mask": draw_pore_mask(jax.random.fold_in(key_of[6], 71), 0),
        "relax_rates": jnp.clip(jax.random.uniform(key_of[3], (19,), jnp.float32, 0.7, 1.8), 0.7, 1.8),
        "window_step": jax.random.randint(key_of[4], (1,), 1, CZ).astype(jnp.int32),
        "start_slab": jax.random.randint(key_of[5], (1,), 0, 1024 * SLABS).astype(jnp.int32),
    }


TRACER_OMEGA = 1.25


def velocity_table():
    return np.array([(0, 0, 0), (1, 0, 0), (-1, 0, 0), (0, 1, 0), (0, -1, 0), (0, 0, 1), (0, 0, -1),
                     (1, 1, 0), (-1, -1, 0), (1, -1, 0), (-1, 1, 0), (1, 0, 1), (-1, 0, -1), (1, 0, -1),
                     (-1, 0, 1), (0, 1, 1), (0, -1, -1), (0, 1, -1), (0, -1, 1)], dtype=np.int32)


def flow_weights():
    return np.array([1.0 / 3.0] + [1.0 / 18.0] * 6 + [1.0 / 36.0] * 12, dtype=np.float32)


def opposite_table():
    return np.array([0, 2, 1, 4, 3, 6, 5, 8, 7, 10, 9, 12, 11, 14, 13, 16, 15, 18, 17], dtype=np.int32)


def tracer_table():
    return np.array([(0, 0, 0), (1, 0, 0), (-1, 0, 0), (0, 1, 0), (0, -1, 0), (0, 0, 1), (0, 0, -1)], dtype=np.int32)


def tracer_weights():
    return np.array([0.25] + [0.125] * 6, dtype=np.float32)


def moment_matrix():
    lattice = velocity_table().astype(np.float32)
    along_x, along_y, along_z = lattice[:, 0], lattice[:, 1], lattice[:, 2]
    speed_sq = along_x * along_x + along_y * along_y + along_z * along_z
    polynomials = [np.ones(19, dtype=np.float32), 19 * speed_sq - 30, (21 * speed_sq * speed_sq - 53 * speed_sq + 24) / 2,
                   along_x, (5 * speed_sq - 9) * along_x, along_y, (5 * speed_sq - 9) * along_y,
                   along_z, (5 * speed_sq - 9) * along_z, 3 * along_x * along_x - speed_sq,
                   (3 * speed_sq - 5) * (3 * along_x * along_x - speed_sq), along_y * along_y - along_z * along_z,
                   (3 * speed_sq - 5) * (along_y * along_y - along_z * along_z), along_x * along_y,
                   along_y * along_z, along_x * along_z, (along_y * along_y - along_z * along_z) * along_x,
                   (along_z * along_z - along_x * along_x) * along_y, (along_x * along_x - along_y * along_y) * along_z]
    return np.stack(polynomials).astype(np.float32)


def collision_kernel(relax_rates):
    moments = moment_matrix()
    row_norms = np.sum(moments * moments, axis=1)
    scaled = jnp.asarray(moments.T, jnp.float32) * (relax_rates / jnp.asarray(row_norms, jnp.float32))[None, :]
    return jnp.dot(scaled, jnp.asarray(moments, jnp.float32), precision=lax.Precision.HIGHEST)


def flow_collide(flow_state, pore_mask, kernel):
    pop_shape = flow_state.shape
    flat_pops = flow_state.reshape(19, -1)
    velocity_rows = jnp.asarray(velocity_table(), jnp.float32)
    density = jnp.sum(flat_pops, axis=0)
    momentum = jnp.dot(velocity_rows.T, flat_pops, precision=lax.Precision.HIGHEST)
    projected = jnp.dot(velocity_rows, momentum, precision=lax.Precision.HIGHEST)
    momentum_sq = jnp.sum(momentum * momentum, axis=0)
    weights = jnp.asarray(flow_weights(), jnp.float32)[:, None]
    equilibrium = weights * (density[None, :] + 3.0 * projected + 4.5 * projected * projected - 1.5 * momentum_sq[None, :])
    relaxed = flat_pops - jnp.dot(kernel, flat_pops - equilibrium, precision=lax.Precision.HIGHEST)
    bounced = flat_pops[opposite_table()]
    open_flat = pore_mask.reshape(1, -1)
    return jnp.where(open_flat == 1, relaxed, bounced).reshape(pop_shape)


def flow_momentum(flow_state, pore_mask):
    flat_pops = flow_state.reshape(19, -1)
    velocity_rows = jnp.asarray(velocity_table(), jnp.float32)
    momentum = jnp.dot(velocity_rows.T, flat_pops, precision=lax.Precision.HIGHEST)
    momentum = momentum * pore_mask.reshape(1, -1).astype(jnp.float32)
    return momentum.reshape((3,) + flow_state.shape[1:])


def stream_flow(relaxed):
    lattice = velocity_table()
    passed = []
    for number in range(19):
        step_x, step_y, step_z = int(lattice[number, 0]), int(lattice[number, 1]), int(lattice[number, 2])
        passed.append(jnp.roll(relaxed[number], (step_z, step_x, step_y), axis=(0, 1, 2)))
    return jnp.stack(passed)


def tracer_collide(tracer_state, window_flow):
    pop_shape = tracer_state.shape
    flat_pops = tracer_state.reshape(7, -1)
    concentration = jnp.sum(flat_pops, axis=0)
    projected = jnp.dot(jnp.asarray(tracer_table(), jnp.float32), window_flow.reshape(3, -1),
                        precision=lax.Precision.HIGHEST)
    weights = jnp.asarray(tracer_weights(), jnp.float32)[:, None]
    equilibrium = weights * concentration[None, :] * (1.0 + 4.0 * projected)
    return (flat_pops - TRACER_OMEGA * (flat_pops - equilibrium)).reshape(pop_shape)


def shift_open(field, step_z):
    if step_z == 0:
        return field
    blank = jnp.zeros_like(field[:1])
    if step_z == 1:
        return jnp.concatenate([blank, field[:-1]], axis=0)
    return jnp.concatenate([field[1:], blank], axis=0)


def stream_tracer(relaxed):
    lattice = tracer_table()
    passed = []
    for number in range(7):
        step_x, step_y, step_z = int(lattice[number, 0]), int(lattice[number, 1]), int(lattice[number, 2])
        moved = jnp.roll(relaxed[number], (step_x, step_y), axis=(1, 2))
        passed.append(shift_open(moved, step_z))
    return jnp.stack(passed)


def reference(flow_pops, tracer_pops, pore_mask, relax_rates, window_step, start_slab):
    kernel = collision_kernel(relax_rates)
    flow_state = flow_pops
    for sweep in range(2):
        flow_state = stream_flow(flow_collide(flow_state, pore_mask, kernel))
    carried = flow_momentum(flow_state, pore_mask)
    offset = (start_slab[0] * CZ + window_step[0]).astype(jnp.int32)
    window_flow = jnp.roll(carried, -offset, axis=1)
    blank = jnp.zeros((7, CZ) + tracer_pops.shape[2:], tracer_pops.dtype)
    tracer_long = jnp.concatenate([tracer_pops, blank], axis=1)
    tracer_state = lax.dynamic_slice_in_dim(tracer_long, window_step[0].astype(jnp.int32), NZ, 1)
    for sweep in range(2):
        tracer_state = stream_tracer(tracer_collide(tracer_state, window_flow))
    return flow_state, tracer_state
```

```python
import jax
import jax.numpy as jnp
import numpy as np
from jax import lax
from jax.experimental import pallas as pl
from jax.experimental.pallas import tpu as pltpu
from jax.sharding import PartitionSpec as P

ROWS = 32
SIDE = 8
LANES = 128
PARAMS = pltpu.CompilerParams(vmem_limit_bytes=20 * 1024 * 1024)

VEL = [
    (0, 0, 0), (1, 0, 0), (-1, 0, 0), (0, 1, 0), (0, -1, 0), (0, 0, 1), (0, 0, -1),
    (1, 1, 0), (-1, -1, 0), (1, -1, 0), (-1, 1, 0), (1, 0, 1), (-1, 0, -1),
    (1, 0, -1), (-1, 0, 1), (0, 1, 1), (0, -1, -1), (0, 1, -1), (0, -1, 1),
]
X_UP = [1, 7, 9, 11, 13]
X_DOWN = [2, 8, 10, 12, 14]
Z_UP = [5, 11, 14, 15, 18]
Z_DOWN = [6, 12, 13, 16, 17]
Z_FLAT = [0, 1, 2, 3, 4, 7, 8, 9, 10]
LOW_PLANE = {(i, 1): n for n, i in enumerate(Z_FLAT + Z_UP)}
LOW_PLANE.update({(i, 2): 14 + n for n, i in enumerate(Z_UP)})
HIGH_PLANE = {(i, 1): n for n, i in enumerate(Z_FLAT + Z_DOWN)}
HIGH_PLANE.update({(i, 2): 14 + n for n, i in enumerate(Z_DOWN)})
PAIRS = [(1, 2), (3, 4), (5, 6), (7, 8), (9, 10), (11, 12), (13, 14), (15, 16), (17, 18)]
NORMS = [19, 2394, 252, 10, 40, 10, 40, 10, 40, 36, 72, 12, 24, 4, 4, 4, 8, 8, 8]


def rates_of(rates_ref):
    return [rates_ref[k] * np.float32(1.0 / NORMS[k]) for k in range(19)]


def collide(f, pore, c):
    e = [f[a] + f[b] for a, b in PAIRS]
    o = [f[a] - f[b] for a, b in PAIRS]
    rho = f[0] + ((e[0] + e[1]) + (e[2] + e[3])) + ((e[4] + e[5]) + (e[6] + e[7]) + e[8])
    jx = o[0] + (o[3] + o[4]) + (o[5] + o[6])
    jy = o[1] + (o[3] - o[4]) + (o[7] + o[8])
    jz = o[2] + (o[5] - o[6]) + (o[7] - o[8])
    xx, yy, zz = jx * jx, jy * jy, jz * jz
    base = rho - 1.5 * (xx + yy + zz)
    axis, diag = base * np.float32(1 / 9), base * np.float32(1 / 18)
    d0 = f[0] - base * np.float32(1 / 3)
    third, sixth = np.float32(1 / 3), np.float32(1 / 6)
    de = [e[0] - (axis + 0.5 * xx), e[1] - (axis + 0.5 * yy), e[2] - (axis + 0.5 * zz)]
    do = [o[0] - third * jx, o[1] - third * jy, o[2] - third * jz]
    for n, p in enumerate((jx + jy, jx - jy, jx + jz, jx - jz, jy + jz, jy - jz)):
        de.append(e[3 + n] - (diag + 0.25 * (p * p)))
        do.append(o[3 + n] - sixth * p)
    a = de[0] + de[1] + de[2]
    pxy, pxz, pyz = de[3] + de[4], de[5] + de[6], de[7] + de[8]
    b = pxy + pxz + pyz
    a9, b9 = 3.0 * de[0] - a, b - 3.0 * pyz
    a11, b11 = de[1] - de[2], pxy - pxz
    sxy, txy = do[3] + do[4], do[3] - do[4]
    sxz, txz = do[5] + do[6], do[5] - do[6]
    syz, tyz = do[7] + do[8], do[7] - do[8]
    restx, resty, restz = sxy + sxz, txy + syz, txz + tyz
    n = [
        c[0] * (d0 + a + b),
        c[1] * (8.0 * b - 11.0 * a - 30.0 * d0),
        c[2] * (12.0 * d0 - 4.0 * a + b),
        c[3] * (do[0] + restx),
        c[4] * (restx - 4.0 * do[0]),
        c[5] * (do[1] + resty),
        c[6] * (resty - 4.0 * do[1]),
        c[7] * (do[2] + restz),
        c[8] * (restz - 4.0 * do[2]),
        c[9] * (a9 + b9),
        c[10] * (b9 - 2.0 * a9),
        c[11] * (a11 + b11),
        c[12] * (b11 - 2.0 * a11),
        c[13] * (de[3] - de[4]),
        c[14] * (de[7] - de[8]),
        c[15] * (de[5] - de[6]),
        c[16] * (sxy - sxz),
        c[17] * (syz - txy),
        c[18] * (txz - tyz),
    ]
    r0 = n[0] - 30.0 * n[1] + 12.0 * n[2]
    ax = n[0] - 11.0 * n[1] - 4.0 * n[2]
    dg = n[0] + 8.0 * n[1] + n[2]
    u, v = n[9] - 2.0 * n[10], n[11] - 2.0 * n[12]
    p, q = n[9] + n[10], n[11] + n[12]
    exy, exz, eyz = dg + p + q, dg + p - q, dg - 2.0 * p
    ev = [ax + 2.0 * u, ax - u + v, ax - u - v, exy + n[13], exy - n[13], exz + n[15], exz - n[15], eyz + n[14], eyz - n[14]]
    gx, gy, gz = n[3] + n[4], n[5] + n[6], n[7] + n[8]
    xa, ya = gx + n[16], gy - n[17]
    xb, zb = gx - n[16], gz + n[18]
    yc, zc = gy + n[17], gz - n[18]
    od = [n[3] - 4.0 * n[4], n[5] - 4.0 * n[6], n[7] - 4.0 * n[8], xa + ya, xa - ya, xb + zb, xb - zb, yc + zc, yc - zc]
    out = [None] * 19
    out[0] = jnp.where(pore, f[0] - r0, f[0])
    for m, (i, k) in enumerate(PAIRS):
        out[i] = jnp.where(pore, f[i] - (ev[m] + od[m]), f[k])
        out[k] = jnp.where(pore, f[k] - (ev[m] - od[m]), f[i])
    return out


def tile(row):
    start = row * SIDE
    if not isinstance(row, int):
        start = pl.multiple_of(start, SIDE)
    return pl.ds(start, SIDE)


def column(side, count=ROWS, first=0):
    return pl.ds(first * SIDE + side, count, stride=SIDE)


def roll_y(value, by):
    return value if by == 0 else pltpu.roll(value, by % LANES, axis=value.ndim - 1)


def roll_x(value, by):
    return value if by == 0 else pltpu.roll(value, by % SIDE, axis=0)


def sublane():
    return lax.broadcasted_iota(jnp.int32, (SIDE, LANES), 0)


def faces_kernel(rates_ref, low_ref, high_ref, mask_low_ref, mask_high_ref, up_ref, down_ref):
    c = rates_of(rates_ref)
    for row, ref, mask_ref in ((0, low_ref, mask_low_ref), (1, low_ref, mask_low_ref), (0, high_ref, mask_high_ref), (1, high_ref, mask_high_ref)):
        pore = mask_ref[tile(row), :]
        post = collide([ref[i, tile(row), :] for i in range(19)], pore == 1, c)
        if ref is low_ref:
            near, out, table = row == 0, down_ref, HIGH_PLANE
        else:
            near, out, table = row == 1, up_ref, LOW_PLANE
        for (i, depth), plane in table.items():
            if (depth == 1) == near:
                out[tile(plane), :] = post[i]
        if near:
            out[tile(19), :] = pore.astype(jnp.float32)


def first_kernel(rates_ref, flow_ref, mask_ref, post_ref, side_ref):
    c = rates_of(rates_ref)

    @pl.loop(0, ROWS)
    def _(row):
        post = collide([flow_ref[i, tile(row), :] for i in range(19)], mask_ref[tile(row), :] == 1, c)
        for i in range(19):
            post_ref[i, tile(row), :] = post[i]

    for k in range(5):
        side_ref[k] = post_ref[X_UP[k], column(7), :]
        side_ref[5 + k] = post_ref[X_DOWN[k], column(0), :]


def pack_kernel(side_ref, low_ref, high_ref, up_ref, down_ref):
    for base, pops, edge, out in ((0, X_UP, 7, up_ref), (5, X_DOWN, 0, down_ref)):
        for k, i in enumerate(pops):
            cz = VEL[i][2]
            out[k, pl.ds(1 + cz, ROWS), :] = side_ref[base + k]
            for spot in range(1 + cz):
                plane = LOW_PLANE[(i, 1 + cz - spot)]
                out[k, pl.ds(spot, 1), :] = low_ref[pl.ds(plane * SIDE + edge, 1), :]
            for spot in range(33 + cz, 34):
                plane = HIGH_PLANE[(i, spot - 32 - cz)]
                out[k, pl.ds(spot, 1), :] = high_ref[pl.ds(plane * SIDE + edge, 1), :]


def second_kernel(rates_ref, post_ref, mask_ref, low_ref, high_ref, xlow_ref, xhigh_ref,
                  out_ref, below_ref, above_ref, up_ref, down_ref, edge_ref):
    c = rates_of(rates_ref)
    for k in range(5):
        edge_ref[k, column(0, 34), :] = xlow_ref[k]
        edge_ref[k, column(7, 34), :] = xhigh_ref[k]
    sub = sublane()
    first, last = sub == 0, sub == SIDE - 1

    def source(i, row):
        if isinstance(row, int) and row < 0:
            return low_ref[tile(LOW_PLANE[(i, -row)]), :]
        if isinstance(row, int) and row >= ROWS:
            return high_ref[tile(HIGH_PLANE[(i, row - ROWS + 1)]), :]
        return post_ref[i, tile(row), :]

    def step(row, pore):
        f = []
        for i, (cx, cy, cz) in enumerate(VEL):
            value = source(i, row - cz)
            if cx == 1:
                value = jnp.where(first, edge_ref[X_UP.index(i), tile(row + 1), :], roll_x(value, 1))
            if cx == -1:
                value = jnp.where(last, edge_ref[X_DOWN.index(i), tile(row + 1), :], roll_x(value, -1))
            f.append(roll_y(value, cy))
        return collide(f, pore, c)

    def inner(row):
        post = step(row, mask_ref[tile(row), :] == 1)
        for i in range(19):
            out_ref[i, tile(row), :] = post[i]

    post = step(-1, low_ref[tile(19), :] == 1.0)
    for k, i in enumerate(Z_UP):
        below_ref[k] = post[i]
    post = step(ROWS, high_ref[tile(19), :] == 1.0)
    for k, i in enumerate(Z_DOWN):
        above_ref[k] = post[i]
    inner(0)
    inner(ROWS - 1)

    @pl.loop(1, ROWS - 1)
    def _(row):
        inner(row)

    for pops, edge, out in ((X_UP, 7, up_ref), (X_DOWN, 0, down_ref)):
        for k, i in enumerate(pops):
            cz = VEL[i][2]
            value = out_ref[i, column(edge), :]
            if cz == 0:
                out[k] = value
            elif cz == 1:
                out[k, pl.ds(1, ROWS - 1), :] = value[: ROWS - 1]
                out[k, pl.ds(0, 1), :] = below_ref[Z_UP.index(i), pl.ds(edge, 1), :]
            else:
                out[k, pl.ds(0, ROWS - 1), :] = value[1:]
                out[k, pl.ds(ROWS - 1, 1), :] = above_ref[Z_DOWN.index(i), pl.ds(edge, 1), :]


def streamed(post_ref, below_ref, above_ref, i, row):
    cx, cy, cz = VEL[i]
    if isinstance(row, int) and row - cz < 0:
        value = below_ref[Z_UP.index(i)]
    elif isinstance(row, int) and row - cz >= ROWS:
        value = above_ref[Z_DOWN.index(i)]
    else:
        value = post_ref[i, tile(row - cz), :]
    return roll_y(roll_x(value, cx), cy)


def momentum_kernel(post_ref, below_ref, above_ref, mask_ref, out_ref):
    sub = sublane()
    not_first, not_last = sub > 0, sub < SIDE - 1

    def inner(row):
        sums = [None, None, None]
        for i in range(1, 19):
            value = streamed(post_ref, below_ref, above_ref, i, row)
            if VEL[i][0] == 1:
                value = jnp.where(not_first, value, 0.0)
            if VEL[i][0] == -1:
                value = jnp.where(not_last, value, 0.0)
            for part in range(3):
                sign = VEL[i][part]
                if sign == 1:
                    sums[part] = value if sums[part] is None else sums[part] + value
                if sign == -1:
                    sums[part] = sums[part] - value
        pore = mask_ref[tile(row), :].astype(jnp.float32)
        for part in range(3):
            out_ref[part, tile(row), :] = sums[part] * pore

    inner(0)
    inner(ROWS - 1)

    @pl.loop(1, ROWS - 1)
    def _(row):
        inner(row)


def carried_kernel(part_ref, mask_ref, xlow_ref, xhigh_ref, out_ref):
    out_ref[...] = part_ref[...]
    for pops, edge, halo in ((X_UP, 0, xlow_ref), (X_DOWN, 7, xhigh_ref)):
        values = [roll_y(halo[k], VEL[i][1]) for k, i in enumerate(pops)]
        pore = mask_ref[column(edge), :].astype(jnp.float32)
        for part in range(3):
            total = None
            for k, i in enumerate(pops):
                sign = VEL[i][part]
                if sign:
                    term = values[k] if sign == 1 else -values[k]
                    total = term if total is None else total + term
            out_ref[part, column(edge), :] = part_ref[part, column(edge), :] + pore * total


def flow_out_kernel(post_ref, below_ref, above_ref, xlow_ref, xhigh_ref, out_ref):
    def inner(row):
        for i in range(19):
            out_ref[i, tile(row), :] = streamed(post_ref, below_ref, above_ref, i, row)

    inner(0)
    inner(ROWS - 1)

    @pl.loop(1, ROWS - 1)
    def _(row):
        inner(row)

    for pops, edge, halo in ((X_UP, 0, xlow_ref), (X_DOWN, 7, xhigh_ref)):
        for k, i in enumerate(pops):
            out_ref[i, column(edge), :] = roll_y(halo[k], VEL[i][1])


def tracer_collide(g, flow):
    total = ((g[0] + g[1]) + (g[2] + g[3])) + ((g[4] + g[5]) + g[6])
    scaled = 0.125 * total
    out = [g[0] - 1.25 * (g[0] - 0.25 * total)]
    for part in range(3):
        lean = 4.0 * flow[part]
        up, down = g[1 + 2 * part], g[2 + 2 * part]
        out.append(up - 1.25 * (up - scaled * (1.0 + lean)))
        out.append(down - 1.25 * (down - scaled * (1.0 - lean)))
    return out


def tracer_first_kernel(info_ref, own_ref, next_ref, far_ref, flow_ref, flow_far_ref, post_ref, up_ref, down_ref):
    shift, offset, keep_low, keep_high = info_ref[0], info_ref[1], info_ref[2], info_ref[3]

    def store(row, g, flow):
        post = tracer_collide(g, flow)
        keep = jnp.where(row < 0, keep_low, jnp.where(row >= ROWS, keep_high, 1)) > 0
        for i in range(7):
            post_ref[i, tile(row + 2), :] = jnp.where(keep, post[i], 0.0)

    def flow_at(row):
        return [flow_ref[part, tile(row + offset), :] for part in range(3)]

    @pl.when(shift == 1)
    def _():
        store(jnp.int32(-2), [far_ref[i] for i in range(7)], [flow_far_ref[p] for p in range(3)])

    @pl.when(shift == 31)
    def _():
        store(jnp.int32(33), [far_ref[i] for i in range(7)], [flow_far_ref[p] for p in range(3)])

    @pl.loop(jnp.maximum(-2, -shift), ROWS - shift)
    def _(row):
        store(row, [own_ref[i, tile(row + shift), :] for i in range(7)], flow_at(row))

    @pl.loop(ROWS - shift, jnp.minimum(ROWS + 2, 2 * ROWS - shift))
    def _(row):
        store(row, [next_ref[i, tile(row + shift - ROWS), :] for i in range(7)], flow_at(row))

    up_ref[...] = post_ref[1, column(7, 34, 1), :]
    down_ref[...] = post_ref[2, column(0, 34, 1), :]


def tracer_streamed(post_ref, i, row, low, high):
    if i == 5:
        return post_ref[5, tile(row - 1), :]
    if i == 6:
        return post_ref[6, tile(row + 1), :]
    value = post_ref[i, tile(row), :]
    sub = sublane()
    if i == 1:
        return jnp.where(sub == 0, low, roll_x(value, 1))
    if i == 2:
        return jnp.where(sub == SIDE - 1, high, roll_x(value, -1))
    return roll_y(value, (0, 0, 0, 1, -1)[i])


def tracer_second_kernel(info_ref, post_ref, xlow_ref, xhigh_ref, flow_ref, out_ref, up_ref, down_ref, edge_ref):
    offset, keep_low, keep_high = info_ref[1], info_ref[2], info_ref[3]
    edge_ref[column(0, 34), :] = xlow_ref[...]
    edge_ref[column(7, 34), :] = xhigh_ref[...]

    @pl.loop(-1, ROWS + 1)
    def _(row):
        edge = edge_ref[tile(row + 1), :]
        g = [tracer_streamed(post_ref, i, row + 2, edge, edge) for i in range(7)]
        post = tracer_collide(g, [flow_ref[part, tile(row + offset), :] for part in range(3)])
        keep = jnp.where(row < 0, keep_low, jnp.where(row >= ROWS, keep_high, 1)) > 0
        for i in range(7):
            out_ref[i, tile(row + 1), :] = jnp.where(keep, post[i], 0.0)

    up_ref[...] = out_ref[1, column(7, ROWS, 1), :]
    down_ref[...] = out_ref[2, column(0, ROWS, 1), :]


def tracer_out_kernel(post_ref, xlow_ref, xhigh_ref, out_ref):
    @pl.loop(0, ROWS)
    def _(row):
        for i in range(7):
            out_ref[i, tile(row), :] = tracer_streamed(post_ref, i, row + 1, 0.0, 0.0)

    out_ref[1, column(0), :] = xlow_ref[...]
    out_ref[2, column(7), :] = xhigh_ref[...]


def call(kernel, outs, args, smem=0, scratch=()):
    vmem = pl.BlockSpec(memory_space=pltpu.VMEM)
    specs = [pl.BlockSpec(memory_space=pltpu.SMEM)] * smem + [vmem] * (len(args) - smem)
    shapes = [jax.ShapeDtypeStruct(s, jnp.float32) for s in outs]
    return pl.pallas_call(
        kernel,
        out_shape=shapes,
        in_specs=specs,
        out_specs=[vmem] * len(shapes),
        scratch_shapes=list(scratch),
        compiler_params=PARAMS,
    )(*args)


def ring(value, axis, by):
    count = lax.axis_size(axis)
    if by % count == 0:
        return value
    return lax.ppermute(value, axis, [(i, (i + by) % count) for i in range(count)])


def line(value, axis, by):
    count = lax.axis_size(axis)
    pairs = [(i, i + by) for i in range(count) if 0 <= i + by < count]
    return lax.ppermute(value, axis, pairs)


def place(carried, tracer_first, tracer_last, shift, start):
    cells = (SIDE, LANES)

    def branch(slab, kind):
        quarter = kind if kind < 4 else (0 if kind == 4 else 3)
        low, high = max(0, 8 * quarter - 2), min(ROWS, 8 * quarter + 9)

        def run(carried, tracer_first, tracer_last):
            a = ring(carried[:, low * SIDE :], "gz", -slab)
            b = ring(carried[:, : high * SIDE], "gz", -slab - 1)
            fill = jnp.zeros((3, (44 - (ROWS - low) - high) * SIDE, LANES), jnp.float32)
            window = jnp.concatenate([a, b, fill], axis=1)
            if kind < 4:
                return window, jnp.zeros((3,) + cells, jnp.float32), jnp.zeros((7,) + cells, jnp.float32)
            if kind == 4:
                far = ring(carried[:, (ROWS - 1) * SIDE :], "gz", 1 - slab)
                return window, far, line(tracer_last, "gz", 1)
            far = ring(carried[:, :SIDE], "gz", -2 - slab)
            return window, far, line(tracer_first, "gz", -2)

        return run

    kind = jnp.where(shift == 1, 4, jnp.where(shift == 31, 5, shift // 8))
    branches = [branch(slab, kind) for slab in range(lax.axis_size("gz")) for kind in range(6)]
    return lax.switch(start * 6 + kind, branches, carried, tracer_first, tracer_last)


def body(flow_pops, tracer_pops, pore_mask, relax_rates, window_step, start_slab):
    cells = ROWS * SIDE
    flow = flow_pops.reshape(19, cells, LANES)
    tracer = tracer_pops.reshape(7, cells, LANES)
    mask = pore_mask.reshape(cells, LANES)
    position, count = lax.axis_index("gz"), lax.axis_size("gz")
    shift = window_step[0]
    start = start_slab[0] % count

    def ends(at, lead):
        if lead:
            return pl.BlockSpec((19, 16, LANES), lambda _: (0, at, 0))
        return pl.BlockSpec((16, LANES), lambda _: (at, 0))

    whole = pl.BlockSpec((160, LANES), lambda _: (0, 0))
    z_up, z_down = pl.pallas_call(
        faces_kernel,
        out_shape=[jax.ShapeDtypeStruct((160, LANES), jnp.float32)] * 2,
        grid=(1,),
        in_specs=[pl.BlockSpec(memory_space=pltpu.SMEM), ends(0, True), ends(15, True), ends(0, False), ends(15, False)],
        out_specs=[whole, whole],
        compiler_params=PARAMS,
    )(relax_rates, flow, flow, mask, mask)
    z_low, z_high = ring(z_up, "gz", 1), ring(z_down, "gz", -1)
    tracer_next = line(tracer, "gz", -1)
    post1, side1 = call(first_kernel, [(19, cells, LANES), (10, ROWS, LANES)], (relax_rates, flow, mask), smem=1)
    up, down = call(pack_kernel, [(5, 34, LANES)] * 2, (side1, z_low, z_high))
    x_low, x_high = ring(up, "gx", 1), ring(down, "gx", -1)
    post2, below, above, up, down = call(
        second_kernel,
        [(19, cells, LANES), (5, SIDE, LANES), (5, SIDE, LANES), (5, ROWS, LANES), (5, ROWS, LANES)],
        (relax_rates, post1, mask, z_low, z_high, x_low, x_high),
        smem=1,
        scratch=[pltpu.VMEM((5, 34 * SIDE, LANES), jnp.float32)],
    )
    x_low, x_high = ring(up, "gx", 1), ring(down, "gx", -1)
    (partial,) = call(momentum_kernel, [(3, cells, LANES)], (post2, below, above, mask))
    (carried,) = call(carried_kernel, [(3, cells, LANES)], (partial, mask, x_low, x_high))
    (flow_out,) = call(flow_out_kernel, [(19, cells, LANES)], (post2, below, above, x_low, x_high))

    first = tracer[:, :SIDE]
    last = tracer[:, (ROWS - 1) * SIDE :]
    window, flow_far, tracer_far = place(carried, first, last, shift, start)
    low = jnp.maximum(0, 8 * (shift // 8) - 2)
    info = jnp.stack(
        [shift, shift - low, (position > 0).astype(jnp.int32), (position < count - 1).astype(jnp.int32)]
    ).astype(jnp.int32)
    post1, up, down = call(
        tracer_first_kernel,
        [(7, 36 * SIDE, LANES), (34, LANES), (34, LANES)],
        (info, tracer, tracer_next, tracer_far, window, flow_far),
        smem=1,
    )
    x_low, x_high = ring(up, "gx", 1), ring(down, "gx", -1)
    post2, up, down = call(
        tracer_second_kernel,
        [(7, 34 * SIDE, LANES), (ROWS, LANES), (ROWS, LANES)],
        (info, post1, x_low, x_high, window),
        smem=1,
        scratch=[pltpu.VMEM((34 * SIDE, LANES), jnp.float32)],
    )
    x_low, x_high = ring(up, "gx", 1), ring(down, "gx", -1)
    (tracer_out,) = call(tracer_out_kernel, [(7, cells, LANES)], (post2, x_low, x_high))
    return flow_out.reshape(flow_pops.shape), tracer_out.reshape(tracer_pops.shape)


def solution(mesh):
    wide = P(None, "gz", "gx", None)
    return jax.shard_map(
        body,
        mesh=mesh,
        in_specs=(wide, wide, P("gz", "gx", None), P(), P(), P()),
        out_specs=(wide, wide),
        check_vma=False,
    )
```

```python
import jax
import jax.numpy as jnp
import numpy as np
from jax import lax
from jax.experimental import pallas as pl
from jax.experimental.pallas import tpu as pltpu
from jax.sharding import PartitionSpec as P

ROWS = 32
SIDE = 8
LANES = 128
CHUNKS = 4
PARAMS = pltpu.CompilerParams(vmem_limit_bytes=12 * 1024 * 1024)

VEL = [
    (0, 0, 0), (1, 0, 0), (-1, 0, 0), (0, 1, 0), (0, -1, 0), (0, 0, 1), (0, 0, -1),
    (1, 1, 0), (-1, -1, 0), (1, -1, 0), (-1, 1, 0), (1, 0, 1), (-1, 0, -1),
    (1, 0, -1), (-1, 0, 1), (0, 1, 1), (0, -1, -1), (0, 1, -1), (0, -1, 1),
]
X_UP = [1, 7, 9, 11, 13]
X_DOWN = [2, 8, 10, 12, 14]
Z_UP = [5, 11, 14, 15, 18]
Z_DOWN = [6, 12, 13, 16, 17]
Z_FLAT = [0, 1, 2, 3, 4, 7, 8, 9, 10]
LOW_PLANE = {(i, 1): n for n, i in enumerate(Z_FLAT + Z_UP)}
LOW_PLANE.update({(i, 2): 14 + n for n, i in enumerate(Z_UP)})
HIGH_PLANE = {(i, 1): n for n, i in enumerate(Z_FLAT + Z_DOWN)}
HIGH_PLANE.update({(i, 2): 14 + n for n, i in enumerate(Z_DOWN)})
PAIRS = [(1, 2), (3, 4), (5, 6), (7, 8), (9, 10), (11, 12), (13, 14), (15, 16), (17, 18)]
NORMS = [19, 2394, 252, 10, 40, 10, 40, 10, 40, 36, 72, 12, 24, 4, 4, 4, 8, 8, 8]


def rates_of(rates_ref):
    return [rates_ref[k] * np.float32(1.0 / NORMS[k]) for k in range(19)]


def collide(f, pore, c):
    e = [f[a] + f[b] for a, b in PAIRS]
    o = [f[a] - f[b] for a, b in PAIRS]
    rho = f[0] + ((e[0] + e[1]) + (e[2] + e[3])) + ((e[4] + e[5]) + (e[6] + e[7]) + e[8])
    jx = o[0] + (o[3] + o[4]) + (o[5] + o[6])
    jy = o[1] + (o[3] - o[4]) + (o[7] + o[8])
    jz = o[2] + (o[5] - o[6]) + (o[7] - o[8])
    xx, yy, zz = jx * jx, jy * jy, jz * jz
    base = rho - 1.5 * (xx + yy + zz)
    axis, diag = base * np.float32(1 / 9), base * np.float32(1 / 18)
    d0 = f[0] - base * np.float32(1 / 3)
    third, sixth = np.float32(1 / 3), np.float32(1 / 6)
    de = [e[0] - (axis + 0.5 * xx), e[1] - (axis + 0.5 * yy), e[2] - (axis + 0.5 * zz)]
    do = [o[0] - third * jx, o[1] - third * jy, o[2] - third * jz]
    for n, p in enumerate((jx + jy, jx - jy, jx + jz, jx - jz, jy + jz, jy - jz)):
        de.append(e[3 + n] - (diag + 0.25 * (p * p)))
        do.append(o[3 + n] - sixth * p)
    a = de[0] + de[1] + de[2]
    pxy, pxz, pyz = de[3] + de[4], de[5] + de[6], de[7] + de[8]
    b = pxy + pxz + pyz
    a9, b9 = 3.0 * de[0] - a, b - 3.0 * pyz
    a11, b11 = de[1] - de[2], pxy - pxz
    sxy, txy = do[3] + do[4], do[3] - do[4]
    sxz, txz = do[5] + do[6], do[5] - do[6]
    syz, tyz = do[7] + do[8], do[7] - do[8]
    restx, resty, restz = sxy + sxz, txy + syz, txz + tyz
    n = [
        c[0] * (d0 + a + b),
        c[1] * (8.0 * b - 11.0 * a - 30.0 * d0),
        c[2] * (12.0 * d0 - 4.0 * a + b),
        c[3] * (do[0] + restx),
        c[4] * (restx - 4.0 * do[0]),
        c[5] * (do[1] + resty),
        c[6] * (resty - 4.0 * do[1]),
        c[7] * (do[2] + restz),
        c[8] * (restz - 4.0 * do[2]),
        c[9] * (a9 + b9),
        c[10] * (b9 - 2.0 * a9),
        c[11] * (a11 + b11),
        c[12] * (b11 - 2.0 * a11),
        c[13] * (de[3] - de[4]),
        c[14] * (de[7] - de[8]),
        c[15] * (de[5] - de[6]),
        c[16] * (sxy - sxz),
        c[17] * (syz - txy),
        c[18] * (txz - tyz),
    ]
    r0 = n[0] - 30.0 * n[1] + 12.0 * n[2]
    ax = n[0] - 11.0 * n[1] - 4.0 * n[2]
    dg = n[0] + 8.0 * n[1] + n[2]
    u, v = n[9] - 2.0 * n[10], n[11] - 2.0 * n[12]
    p, q = n[9] + n[10], n[11] + n[12]
    exy, exz, eyz = dg + p + q, dg + p - q, dg - 2.0 * p
    ev = [ax + 2.0 * u, ax - u + v, ax - u - v, exy + n[13], exy - n[13], exz + n[15], exz - n[15], eyz + n[14], eyz - n[14]]
    gx, gy, gz = n[3] + n[4], n[5] + n[6], n[7] + n[8]
    xa, ya = gx + n[16], gy - n[17]
    xb, zb = gx - n[16], gz + n[18]
    yc, zc = gy + n[17], gz - n[18]
    od = [n[3] - 4.0 * n[4], n[5] - 4.0 * n[6], n[7] - 4.0 * n[8], xa + ya, xa - ya, xb + zb, xb - zb, yc + zc, yc - zc]
    out = [None] * 19
    out[0] = jnp.where(pore, f[0] - r0, f[0])
    for m, (i, k) in enumerate(PAIRS):
        out[i] = jnp.where(pore, f[i] - (ev[m] + od[m]), f[k])
        out[k] = jnp.where(pore, f[k] - (ev[m] - od[m]), f[i])
    return out


def tile(row):
    start = row * SIDE
    if not isinstance(row, int):
        start = pl.multiple_of(start, SIDE)
    return pl.ds(start, SIDE)


def column(side, count=ROWS, first=0):
    return pl.ds(first * SIDE + side, count, stride=SIDE)


def roll_y(value, by):
    return value if by == 0 else pltpu.roll(value, by % LANES, axis=value.ndim - 1)


def roll_x(value, by):
    return value if by == 0 else pltpu.roll(value, by % SIDE, axis=0)


def sublane():
    return lax.broadcasted_iota(jnp.int32, (SIDE, LANES), 0)


def fetch(pairs, sems, first=0):
    copies = [pltpu.make_async_copy(src, dst, sems.at[first + n]) for n, (src, dst) in enumerate(pairs)]
    for copy in copies:
        copy.start()
    return copies


def halves(ref):
    span = ROWS * SIDE // CHUNKS
    parts = [pl.ds(n * span, span) for n in range(CHUNKS)]
    return [ref.at[:, part, :] for part in parts]


def first_kernel(start_ref, kind_ref, rates_ref, flow_ref, mask_ref, up_ref, down_ref, post_ref, side_ref, held_ref, pore_ref, sems):
    del start_ref, kind_ref
    copies = fetch([(mask_ref, pore_ref)] + list(zip(halves(flow_ref), halves(held_ref))), sems)
    c = rates_of(rates_ref)
    copies[0].wait()
    for n in range(CHUNKS):
        copies[1 + n].wait()

        @pl.loop(n * ROWS // CHUNKS, (n + 1) * ROWS // CHUNKS)
        def _(row):
            post = collide([held_ref[i, tile(row), :] for i in range(19)], pore_ref[tile(row), :] == 1, c)
            for i in range(19):
                post_ref[i, tile(row), :] = post[i]

    for near, away, out, table in ((0, 1, down_ref, HIGH_PLANE), (ROWS - 1, ROWS - 2, up_ref, LOW_PLANE)):
        for (i, depth), plane in table.items():
            out[tile(plane), :] = post_ref[i, tile(near if depth == 1 else away), :]
        out[tile(19), :] = pore_ref[tile(near), :].astype(jnp.float32)
    for k in range(5):
        side_ref[k] = post_ref[X_UP[k], column(7), :]
        side_ref[5 + k] = post_ref[X_DOWN[k], column(0), :]


def pack_kernel(side_ref, low_ref, high_ref, up_ref, down_ref):
    for base, pops, edge, out in ((0, X_UP, 7, up_ref), (5, X_DOWN, 0, down_ref)):
        for k, i in enumerate(pops):
            cz = VEL[i][2]
            out[k, pl.ds(1 + cz, ROWS), :] = side_ref[base + k]
            for spot in range(1 + cz):
                plane = LOW_PLANE[(i, 1 + cz - spot)]
                out[k, pl.ds(spot, 1), :] = low_ref[pl.ds(plane * SIDE + edge, 1), :]
            for spot in range(33 + cz, 34):
                plane = HIGH_PLANE[(i, spot - 32 - cz)]
                out[k, pl.ds(spot, 1), :] = high_ref[pl.ds(plane * SIDE + edge, 1), :]


def second_kernel(rates_ref, post_ref, mask_ref, low_ref, high_ref, xlow_ref, xhigh_ref,
                  out_ref, below_ref, above_ref, up_ref, down_ref, edge_ref):
    c = rates_of(rates_ref)
    for k in range(5):
        edge_ref[k, column(0, 34), :] = xlow_ref[k]
        edge_ref[k, column(7, 34), :] = xhigh_ref[k]
    sub = sublane()
    first, last = sub == 0, sub == SIDE - 1

    def source(i, row):
        if isinstance(row, int) and row < 0:
            return low_ref[tile(LOW_PLANE[(i, -row)]), :]
        if isinstance(row, int) and row >= ROWS:
            return high_ref[tile(HIGH_PLANE[(i, row - ROWS + 1)]), :]
        return post_ref[i, tile(row), :]

    def step(row, pore):
        f = []
        for i, (cx, cy, cz) in enumerate(VEL):
            value = source(i, row - cz)
            if cx == 1:
                value = jnp.where(first, edge_ref[X_UP.index(i), tile(row + 1), :], roll_x(value, 1))
            if cx == -1:
                value = jnp.where(last, edge_ref[X_DOWN.index(i), tile(row + 1), :], roll_x(value, -1))
            f.append(roll_y(value, cy))
        return collide(f, pore, c)

    def inner(row):
        post = step(row, mask_ref[tile(row), :] == 1)
        for i in range(19):
            out_ref[i, tile(row), :] = post[i]

    post = step(-1, low_ref[tile(19), :] == 1.0)
    for k, i in enumerate(Z_UP):
        below_ref[k] = post[i]
    post = step(ROWS, high_ref[tile(19), :] == 1.0)
    for k, i in enumerate(Z_DOWN):
        above_ref[k] = post[i]
    inner(0)
    inner(ROWS - 1)

    @pl.loop(1, ROWS - 1, unroll=2)
    def _(row):
        inner(row)

    for pops, edge, out in ((X_UP, 7, up_ref), (X_DOWN, 0, down_ref)):
        for k, i in enumerate(pops):
            cz = VEL[i][2]
            value = out_ref[i, column(edge), :]
            if cz == 0:
                out[k] = value
            elif cz == 1:
                out[k, pl.ds(1, ROWS - 1), :] = value[: ROWS - 1]
                out[k, pl.ds(0, 1), :] = below_ref[Z_UP.index(i), pl.ds(edge, 1), :]
            else:
                out[k, pl.ds(0, ROWS - 1), :] = value[1:]
                out[k, pl.ds(ROWS - 1, 1), :] = above_ref[Z_DOWN.index(i), pl.ds(edge, 1), :]


def streamed(post_ref, below_ref, above_ref, i, row):
    cx, cy, cz = VEL[i]
    if isinstance(row, int) and row - cz < 0:
        value = below_ref[Z_UP.index(i)]
    elif isinstance(row, int) and row - cz >= ROWS:
        value = above_ref[Z_DOWN.index(i)]
    else:
        value = post_ref[i, tile(row - cz), :]
    return roll_y(roll_x(value, cx), cy)


def momentum_kernel(post_ref, below_ref, above_ref, mask_ref, out_ref):
    sub = sublane()
    not_first, not_last = sub > 0, sub < SIDE - 1

    def inner(row):
        sums = [None, None, None]
        for i in range(1, 19):
            value = streamed(post_ref, below_ref, above_ref, i, row)
            if VEL[i][0] == 1:
                value = jnp.where(not_first, value, 0.0)
            if VEL[i][0] == -1:
                value = jnp.where(not_last, value, 0.0)
            for part in range(3):
                sign = VEL[i][part]
                if sign == 1:
                    sums[part] = value if sums[part] is None else sums[part] + value
                if sign == -1:
                    sums[part] = sums[part] - value
        pore = mask_ref[tile(row), :].astype(jnp.float32)
        for part in range(3):
            out_ref[part, tile(row), :] = sums[part] * pore

    inner(0)
    inner(ROWS - 1)

    @pl.loop(1, ROWS - 1, unroll=2)
    def _(row):
        inner(row)


def carried_kernel(part_ref, mask_ref, xlow_ref, xhigh_ref, out_ref):
    out_ref[...] = part_ref[...]
    for pops, edge, halo in ((X_UP, 0, xlow_ref), (X_DOWN, 7, xhigh_ref)):
        values = [roll_y(halo[k], VEL[i][1]) for k, i in enumerate(pops)]
        pore = mask_ref[column(edge), :].astype(jnp.float32)
        for part in range(3):
            total = None
            for k, i in enumerate(pops):
                sign = VEL[i][part]
                if sign:
                    term = values[k] if sign == 1 else -values[k]
                    total = term if total is None else total + term
            out_ref[part, column(edge), :] = part_ref[part, column(edge), :] + pore * total


def flow_out_kernel(post_ref, below_ref, above_ref, xlow_ref, xhigh_ref, out_ref):
    def inner(row):
        for i in range(19):
            out_ref[i, tile(row), :] = streamed(post_ref, below_ref, above_ref, i, row)

    inner(0)
    inner(ROWS - 1)

    @pl.loop(1, ROWS - 1, unroll=2)
    def _(row):
        inner(row)

    for pops, edge, halo in ((X_UP, 0, xlow_ref), (X_DOWN, 7, xhigh_ref)):
        for k, i in enumerate(pops):
            out_ref[i, column(edge), :] = roll_y(halo[k], VEL[i][1])


def tracer_collide(g, flow):
    total = ((g[0] + g[1]) + (g[2] + g[3])) + ((g[4] + g[5]) + g[6])
    scaled = 0.125 * total
    out = [g[0] - 1.25 * (g[0] - 0.25 * total)]
    for part in range(3):
        lean = 4.0 * flow[part]
        up, down = g[1 + 2 * part], g[2 + 2 * part]
        out.append(up - 1.25 * (up - scaled * (1.0 + lean)))
        out.append(down - 1.25 * (down - scaled * (1.0 - lean)))
    return out


def inside():
    position = lax.axis_index("gz")
    return (position > 0).astype(jnp.int32), (position < lax.axis_size("gz") - 1).astype(jnp.int32)


def tracer_first_kernel(shift_ref, own_ref, next_ref, far_ref, here_ref, beyond_ref, post_ref, flow_ref, up_ref, down_ref):
    shift = shift_ref[0]
    keep_low, keep_high = inside()

    def store(row, g, flow):
        post = tracer_collide(g, flow)
        keep = jnp.where(row < 0, keep_low, jnp.where(row >= ROWS, keep_high, 1)) > 0
        for i in range(7):
            post_ref[i, tile(row + 2), :] = jnp.where(keep, post[i], 0.0)
        for part in range(3):
            flow_ref[part, tile(row + 2), :] = flow[part]

    def far(row):
        store(jnp.int32(row), [far_ref[3 + i] for i in range(7)], [far_ref[p] for p in range(3)])

    pl.when(shift == 1)(lambda: far(-2))
    pl.when(shift == ROWS - 1)(lambda: far(ROWS + 1))

    @pl.loop(jnp.maximum(-2, -shift), ROWS - shift)
    def _(row):
        at = tile(row + shift)
        store(row, [own_ref[i, at, :] for i in range(7)], [here_ref[p, at, :] for p in range(3)])

    @pl.loop(ROWS - shift, jnp.minimum(ROWS + 2, 2 * ROWS - shift))
    def _(row):
        at = tile(row + shift - ROWS)
        store(row, [next_ref[i, at, :] for i in range(7)], [beyond_ref[p, at, :] for p in range(3)])

    up_ref[...] = post_ref[1, column(7, 34, 1), :]
    down_ref[...] = post_ref[2, column(0, 34, 1), :]


def tracer_streamed(post_ref, i, row, low, high):
    if i == 5:
        return post_ref[5, tile(row - 1), :]
    if i == 6:
        return post_ref[6, tile(row + 1), :]
    value = post_ref[i, tile(row), :]
    sub = sublane()
    if i == 1:
        return jnp.where(sub == 0, low, roll_x(value, 1))
    if i == 2:
        return jnp.where(sub == SIDE - 1, high, roll_x(value, -1))
    return roll_y(value, (0, 0, 0, 1, -1)[i])


def tracer_second_kernel(post_ref, xlow_ref, xhigh_ref, flow_ref, out_ref, up_ref, down_ref, edge_ref):
    keep_low, keep_high = inside()
    edge_ref[column(0, 34), :] = xlow_ref[...]
    edge_ref[column(7, 34), :] = xhigh_ref[...]

    @pl.loop(-1, ROWS + 1, unroll=2)
    def _(row):
        edge = edge_ref[tile(row + 1), :]
        g = [tracer_streamed(post_ref, i, row + 2, edge, edge) for i in range(7)]
        post = tracer_collide(g, [flow_ref[part, tile(row + 2), :] for part in range(3)])
        keep = jnp.where(row < 0, keep_low, jnp.where(row >= ROWS, keep_high, 1)) > 0
        for i in range(7):
            out_ref[i, tile(row + 1), :] = jnp.where(keep, post[i], 0.0)

    up_ref[...] = out_ref[1, column(7, ROWS, 1), :]
    down_ref[...] = out_ref[2, column(0, ROWS, 1), :]


def tracer_out_kernel(post_ref, xlow_ref, xhigh_ref, out_ref):
    @pl.loop(0, ROWS, unroll=4)
    def _(row):
        for i in range(7):
            out_ref[i, tile(row), :] = tracer_streamed(post_ref, i, row + 1, 0.0, 0.0)

    out_ref[1, column(0), :] = xlow_ref[...]
    out_ref[2, column(7), :] = xhigh_ref[...]


VMEM = pl.BlockSpec(memory_space=pltpu.VMEM)
SMEM = pl.BlockSpec(memory_space=pltpu.SMEM)
ANY = pl.BlockSpec(memory_space=pl.ANY)
HBM = pl.BlockSpec(memory_space=pltpu.HBM)


def hold(value):
    return pltpu.with_memory_space_constraint(value, pltpu.HBM)


def room(*shape, dtype=jnp.float32):
    return pltpu.VMEM(shape, dtype)


def call(kernel, outs, args, specs=None, scratch=(), out_specs=None):
    shapes = [jax.ShapeDtypeStruct(s, jnp.float32) for s in outs]
    return pl.pallas_call(
        kernel,
        out_shape=shapes,
        in_specs=specs or [VMEM] * len(args),
        out_specs=out_specs or [VMEM] * len(shapes),
        scratch_shapes=list(scratch),
        compiler_params=PARAMS,
    )(*args)


def ring(value, axis, by):
    count = lax.axis_size(axis)
    if by % count == 0:
        return value
    return lax.ppermute(value, axis, [(i, (i + by) % count) for i in range(count)])


def line(value, axis, by):
    count = lax.axis_size(axis)
    pairs = [(i, i + by) for i in range(count) if 0 <= i + by < count]
    return lax.ppermute(value, axis, pairs)


def place(carried, start):
    def branch(slab):
        def run(carried):
            return ring(carried, "gz", -slab), ring(carried, "gz", -slab - 1)

        return run

    return lax.switch(start, [branch(slab) for slab in range(lax.axis_size("gz"))], carried)


def far_rows(here, beyond, tracer, kind):
    first, last = slice(0, SIDE), slice((ROWS - 1) * SIDE, ROWS * SIDE)

    def none(here, beyond, tracer):
        return jnp.zeros((10, SIDE, LANES), jnp.float32)

    def before(here, beyond, tracer):
        return jnp.concatenate([ring(here[:, last], "gz", 1), line(tracer[:, last], "gz", 1)])

    def after(here, beyond, tracer):
        return jnp.concatenate([ring(beyond[:, first], "gz", -1), line(tracer[:, first], "gz", -2)])

    return lax.switch(kind[0], [none, before, after], here, beyond, tracer)


def body(flow_pops, tracer_pops, pore_mask, relax_rates, window_step, start_slab):
    cells = ROWS * SIDE
    flow = flow_pops.reshape(19, cells, LANES)
    tracer = tracer_pops.reshape(7, cells, LANES)
    mask = pore_mask.reshape(cells, LANES)
    count = lax.axis_size("gz")

    face, block = (160, LANES), (19, cells, LANES)
    kind = jnp.where(window_step == 1, 1, jnp.where(window_step == ROWS - 1, 2, 0))
    start = lax.clamp(jnp.int32(0), lax.rem(start_slab[0], jnp.int32(count)), jnp.int32(count - 1))
    z_up, z_down, post1, side1 = call(
        first_kernel,
        [face, face, block, (10, ROWS, LANES)],
        (start.reshape(1), kind, relax_rates, hold(flow), hold(mask)),
        [SMEM, SMEM, SMEM, HBM, HBM],
        [room(*block), room(cells, LANES, dtype=jnp.int32), pltpu.SemaphoreType.DMA((1 + CHUNKS,))],
    )
    z_low, z_high = ring(z_up, "gz", 1), ring(z_down, "gz", -1)
    tracer_next = line(tracer, "gz", -1)
    up, down = call(pack_kernel, [(5, 34, LANES)] * 2, (side1, z_low, z_high))
    x_low, x_high = ring(up, "gx", 1), ring(down, "gx", -1)
    post2, below, above, up, down = call(
        second_kernel,
        [block, (5, SIDE, LANES), (5, SIDE, LANES), (5, ROWS, LANES), (5, ROWS, LANES)],
        (relax_rates, post1, mask, z_low, z_high, x_low, x_high),
        [SMEM] + [VMEM] * 6,
        [room(5, 34 * SIDE, LANES)],
    )
    x_low, x_high = ring(up, "gx", 1), ring(down, "gx", -1)
    (partial,) = call(momentum_kernel, [(3, cells, LANES)], (post2, below, above, mask))
    (carried,) = call(carried_kernel, [(3, cells, LANES)], (partial, mask, x_low, x_high))
    (flow_out,) = call(flow_out_kernel, [block], (post2, below, above, x_low, x_high))
    here, beyond = place(carried, start)
    far = far_rows(here, beyond, tracer, kind)
    post1, window, up, down = call(
        tracer_first_kernel,
        [(7, 36 * SIDE, LANES), (3, 36 * SIDE, LANES), (34, LANES), (34, LANES)],
        (window_step, tracer, tracer_next, far, here, beyond),
        [SMEM] + [VMEM] * 5,
    )
    x_low, x_high = ring(up, "gx", 1), ring(down, "gx", -1)
    post2, up, down = call(
        tracer_second_kernel,
        [(7, 34 * SIDE, LANES), (ROWS, LANES), (ROWS, LANES)],
        (post1, x_low, x_high, window),
        [VMEM] * 4,
        [room(34 * SIDE, LANES)],
    )
    x_low, x_high = ring(up, "gx", 1), ring(down, "gx", -1)
    (tracer_out,) = call(tracer_out_kernel, [(7, cells, LANES)], (post2, x_low, x_high))
    return flow_out.reshape(flow_pops.shape), tracer_out.reshape(tracer_pops.shape)


def solution(mesh):
    wide = P(None, "gz", "gx", None)
    return jax.shard_map(
        body,
        mesh=mesh,
        in_specs=(wide, wide, P("gz", "gx", None), P(), P(), P()),
        out_specs=(wide, wide),
        check_vma=False,
    )
```

```python
import jax
import jax.numpy as jnp
import numpy as np
from jax import lax
from jax.experimental import pallas as pl
from jax.experimental.pallas import tpu as pltpu
from jax.sharding import PartitionSpec as P

ROWS = 32
SIDE = 8
LANES = 128
CHUNKS = 4
PARAMS = pltpu.CompilerParams(vmem_limit_bytes=12 * 1024 * 1024)

VEL = [
    (0, 0, 0), (1, 0, 0), (-1, 0, 0), (0, 1, 0), (0, -1, 0), (0, 0, 1), (0, 0, -1),
    (1, 1, 0), (-1, -1, 0), (1, -1, 0), (-1, 1, 0), (1, 0, 1), (-1, 0, -1),
    (1, 0, -1), (-1, 0, 1), (0, 1, 1), (0, -1, -1), (0, 1, -1), (0, -1, 1),
]
X_UP = [1, 7, 9, 11, 13]
X_DOWN = [2, 8, 10, 12, 14]
Z_UP = [5, 11, 14, 15, 18]
Z_DOWN = [6, 12, 13, 16, 17]
Z_FLAT = [0, 1, 2, 3, 4, 7, 8, 9, 10]
LOW_PLANE = {(i, 1): n for n, i in enumerate(Z_FLAT + Z_UP)}
LOW_PLANE.update({(i, 2): 14 + n for n, i in enumerate(Z_UP)})
HIGH_PLANE = {(i, 1): n for n, i in enumerate(Z_FLAT + Z_DOWN)}
HIGH_PLANE.update({(i, 2): 14 + n for n, i in enumerate(Z_DOWN)})
PAIRS = [(1, 2), (3, 4), (5, 6), (7, 8), (9, 10), (11, 12), (13, 14), (15, 16), (17, 18)]
NORMS = [19, 2394, 252, 10, 40, 10, 40, 10, 40, 36, 72, 12, 24, 4, 4, 4, 8, 8, 8]


def rates_of(rates_ref):
    return [rates_ref[k] * np.float32(1.0 / NORMS[k]) for k in range(19)]


def collide(f, pore, c):
    e = [f[a] + f[b] for a, b in PAIRS]
    o = [f[a] - f[b] for a, b in PAIRS]
    rho = f[0] + ((e[0] + e[1]) + (e[2] + e[3])) + ((e[4] + e[5]) + (e[6] + e[7]) + e[8])
    jx = o[0] + (o[3] + o[4]) + (o[5] + o[6])
    jy = o[1] + (o[3] - o[4]) + (o[7] + o[8])
    jz = o[2] + (o[5] - o[6]) + (o[7] - o[8])
    xx, yy, zz = jx * jx, jy * jy, jz * jz
    base = rho - 1.5 * (xx + yy + zz)
    axis, diag = base * np.float32(1 / 9), base * np.float32(1 / 18)
    d0 = f[0] - base * np.float32(1 / 3)
    third, sixth = np.float32(1 / 3), np.float32(1 / 6)
    de = [e[0] - (axis + 0.5 * xx), e[1] - (axis + 0.5 * yy), e[2] - (axis + 0.5 * zz)]
    do = [o[0] - third * jx, o[1] - third * jy, o[2] - third * jz]
    for n, p in enumerate((jx + jy, jx - jy, jx + jz, jx - jz, jy + jz, jy - jz)):
        de.append(e[3 + n] - (diag + 0.25 * (p * p)))
        do.append(o[3 + n] - sixth * p)
    a = de[0] + de[1] + de[2]
    pxy, pxz, pyz = de[3] + de[4], de[5] + de[6], de[7] + de[8]
    b = pxy + pxz + pyz
    a9, b9 = 3.0 * de[0] - a, b - 3.0 * pyz
    a11, b11 = de[1] - de[2], pxy - pxz
    sxy, txy = do[3] + do[4], do[3] - do[4]
    sxz, txz = do[5] + do[6], do[5] - do[6]
    syz, tyz = do[7] + do[8], do[7] - do[8]
    restx, resty, restz = sxy + sxz, txy + syz, txz + tyz
    n = [
        c[0] * (d0 + a + b),
        c[1] * (8.0 * b - 11.0 * a - 30.0 * d0),
        c[2] * (12.0 * d0 - 4.0 * a + b),
        c[3] * (do[0] + restx),
        c[4] * (restx - 4.0 * do[0]),
        c[5] * (do[1] + resty),
        c[6] * (resty - 4.0 * do[1]),
        c[7] * (do[2] + restz),
        c[8] * (restz - 4.0 * do[2]),
        c[9] * (a9 + b9),
        c[10] * (b9 - 2.0 * a9),
        c[11] * (a11 + b11),
        c[12] * (b11 - 2.0 * a11),
        c[13] * (de[3] - de[4]),
        c[14] * (de[7] - de[8]),
        c[15] * (de[5] - de[6]),
        c[16] * (sxy - sxz),
        c[17] * (syz - txy),
        c[18] * (txz - tyz),
    ]
    r0 = n[0] - 30.0 * n[1] + 12.0 * n[2]
    ax = n[0] - 11.0 * n[1] - 4.0 * n[2]
    dg = n[0] + 8.0 * n[1] + n[2]
    u, v = n[9] - 2.0 * n[10], n[11] - 2.0 * n[12]
    p, q = n[9] + n[10], n[11] + n[12]
    exy, exz, eyz = dg + p + q, dg + p - q, dg - 2.0 * p
    ev = [ax + 2.0 * u, ax - u + v, ax - u - v, exy + n[13], exy - n[13], exz + n[15], exz - n[15], eyz + n[14], eyz - n[14]]
    gx, gy, gz = n[3] + n[4], n[5] + n[6], n[7] + n[8]
    xa, ya = gx + n[16], gy - n[17]
    xb, zb = gx - n[16], gz + n[18]
    yc, zc = gy + n[17], gz - n[18]
    od = [n[3] - 4.0 * n[4], n[5] - 4.0 * n[6], n[7] - 4.0 * n[8], xa + ya, xa - ya, xb + zb, xb - zb, yc + zc, yc - zc]
    out = [None] * 19
    out[0] = jnp.where(pore, f[0] - r0, f[0])
    for m, (i, k) in enumerate(PAIRS):
        out[i] = jnp.where(pore, f[i] - (ev[m] + od[m]), f[k])
        out[k] = jnp.where(pore, f[k] - (ev[m] - od[m]), f[i])
    return out


def tile(row):
    start = row * SIDE
    if not isinstance(row, int):
        start = pl.multiple_of(start, SIDE)
    return pl.ds(start, SIDE)


def column(side, count=ROWS, first=0):
    return pl.ds(first * SIDE + side, count, stride=SIDE)


def roll_y(value, by):
    return value if by == 0 else pltpu.roll(value, by % LANES, axis=value.ndim - 1)


def roll_x(value, by):
    return value if by == 0 else pltpu.roll(value, by % SIDE, axis=0)


def sublane():
    return lax.broadcasted_iota(jnp.int32, (SIDE, LANES), 0)


def fetch(pairs, sems, first=0):
    copies = [pltpu.make_async_copy(src, dst, sems.at[first + n]) for n, (src, dst) in enumerate(pairs)]
    for copy in copies:
        copy.start()
    return copies


def halves(ref):
    span = ROWS * SIDE // CHUNKS
    parts = [pl.ds(n * span, span) for n in range(CHUNKS)]
    return [ref.at[:, part, :] for part in parts]


def faces_kernel(start_ref, kind_ref, rates_ref, flow_ref, mask_ref, up_ref, down_ref, pops_ref, pore_ref, sems):
    del start_ref, kind_ref
    ends = (pl.ds(0, 2 * SIDE), pl.ds((ROWS - 2) * SIDE, 2 * SIDE))
    pairs = [(flow_ref.at[:, end, :], pops_ref.at[n]) for n, end in enumerate(ends)]
    pairs += [(mask_ref.at[end, :], pore_ref.at[n]) for n, end in enumerate(ends)]
    copies = fetch(pairs, sems)
    c = rates_of(rates_ref)
    for copy in copies:
        copy.wait()
    for end, out, table in ((0, down_ref, HIGH_PLANE), (1, up_ref, LOW_PLANE)):
        for row in range(2):
            near = row == end
            pore = pore_ref[end, tile(row), :]
            post = collide([pops_ref[end, i, tile(row), :] for i in range(19)], pore == 1, c)
            for (i, depth), plane in table.items():
                if (depth == 1) == near:
                    out[tile(plane), :] = post[i]
            if near:
                out[tile(19), :] = pore.astype(jnp.float32)


def first_kernel(rates_ref, flow_ref, mask_ref, post_ref, side_ref, held_ref, pore_ref, sems):
    copies = fetch([(mask_ref, pore_ref)] + list(zip(halves(flow_ref), halves(held_ref))), sems)
    c = rates_of(rates_ref)
    copies[0].wait()
    for n in range(CHUNKS):
        copies[1 + n].wait()

        @pl.loop(n * ROWS // CHUNKS, (n + 1) * ROWS // CHUNKS)
        def _(row):
            post = collide([held_ref[i, tile(row), :] for i in range(19)], pore_ref[tile(row), :] == 1, c)
            for i in range(19):
                post_ref[i, tile(row), :] = post[i]

    for k in range(5):
        side_ref[k] = post_ref[X_UP[k], column(7), :]
        side_ref[5 + k] = post_ref[X_DOWN[k], column(0), :]


def pack_kernel(side_ref, low_ref, high_ref, up_ref, down_ref):
    for base, pops, edge, out in ((0, X_UP, 7, up_ref), (5, X_DOWN, 0, down_ref)):
        for k, i in enumerate(pops):
            cz = VEL[i][2]
            out[k, pl.ds(1 + cz, ROWS), :] = side_ref[base + k]
            for spot in range(1 + cz):
                plane = LOW_PLANE[(i, 1 + cz - spot)]
                out[k, pl.ds(spot, 1), :] = low_ref[pl.ds(plane * SIDE + edge, 1), :]
            for spot in range(33 + cz, 34):
                plane = HIGH_PLANE[(i, spot - 32 - cz)]
                out[k, pl.ds(spot, 1), :] = high_ref[pl.ds(plane * SIDE + edge, 1), :]


def second_kernel(rates_ref, post_ref, mask_ref, low_ref, high_ref, xlow_ref, xhigh_ref, tracer_up_ref, tracer_down_ref,
                  out_ref, below_ref, above_ref, up_ref, down_ref, edge_ref):
    c = rates_of(rates_ref)
    for k in range(5):
        edge_ref[k, column(0, 34), :] = xlow_ref[k]
        edge_ref[k, column(7, 34), :] = xhigh_ref[k]
    sub = sublane()
    first, last = sub == 0, sub == SIDE - 1

    def source(i, row):
        if isinstance(row, int) and row < 0:
            return low_ref[tile(LOW_PLANE[(i, -row)]), :]
        if isinstance(row, int) and row >= ROWS:
            return high_ref[tile(HIGH_PLANE[(i, row - ROWS + 1)]), :]
        return post_ref[i, tile(row), :]

    def step(row, pore):
        f = []
        for i, (cx, cy, cz) in enumerate(VEL):
            value = source(i, row - cz)
            if cx == 1:
                value = jnp.where(first, edge_ref[X_UP.index(i), tile(row + 1), :], roll_x(value, 1))
            if cx == -1:
                value = jnp.where(last, edge_ref[X_DOWN.index(i), tile(row + 1), :], roll_x(value, -1))
            f.append(roll_y(value, cy))
        return collide(f, pore, c)

    def inner(row):
        post = step(row, mask_ref[tile(row), :] == 1)
        for i in range(19):
            out_ref[i, tile(row), :] = post[i]

    post = step(-1, low_ref[tile(19), :] == 1.0)
    for k, i in enumerate(Z_UP):
        below_ref[k] = post[i]
    post = step(ROWS, high_ref[tile(19), :] == 1.0)
    for k, i in enumerate(Z_DOWN):
        above_ref[k] = post[i]
    inner(0)
    inner(ROWS - 1)

    @pl.loop(1, ROWS - 1, unroll=2)
    def _(row):
        inner(row)

    for pops, edge, out, tracer_ref in ((X_UP, 7, up_ref, tracer_up_ref), (X_DOWN, 0, down_ref, tracer_down_ref)):
        out[pl.ds(5, 5)] = tracer_ref[...]
        for k, i in enumerate(pops):
            out[k, pl.ds(ROWS, 2), :] = jnp.zeros((2, LANES), jnp.float32)
            cz = VEL[i][2]
            value = out_ref[i, column(edge), :]
            if cz == 0:
                out[k, pl.ds(0, ROWS), :] = value
            elif cz == 1:
                out[k, pl.ds(1, ROWS - 1), :] = value[: ROWS - 1]
                out[k, pl.ds(0, 1), :] = below_ref[Z_UP.index(i), pl.ds(edge, 1), :]
            else:
                out[k, pl.ds(0, ROWS - 1), :] = value[1:]
                out[k, pl.ds(ROWS - 1, 1), :] = above_ref[Z_DOWN.index(i), pl.ds(edge, 1), :]


def streamed(post_ref, below_ref, above_ref, i, row):
    cx, cy, cz = VEL[i]
    if isinstance(row, int) and row - cz < 0:
        value = below_ref[Z_UP.index(i)]
    elif isinstance(row, int) and row - cz >= ROWS:
        value = above_ref[Z_DOWN.index(i)]
    else:
        value = post_ref[i, tile(row - cz), :]
    return roll_y(roll_x(value, cx), cy)


def momentum_kernel(post_ref, below_ref, above_ref, mask_ref, out_ref):
    sub = sublane()
    not_first, not_last = sub > 0, sub < SIDE - 1

    def inner(row):
        sums = [None, None, None]
        for i in range(1, 19):
            value = streamed(post_ref, below_ref, above_ref, i, row)
            if VEL[i][0] == 1:
                value = jnp.where(not_first, value, 0.0)
            if VEL[i][0] == -1:
                value = jnp.where(not_last, value, 0.0)
            for part in range(3):
                sign = VEL[i][part]
                if sign == 1:
                    sums[part] = value if sums[part] is None else sums[part] + value
                if sign == -1:
                    sums[part] = sums[part] - value
        pore = mask_ref[tile(row), :].astype(jnp.float32)
        for part in range(3):
            out_ref[part, tile(row), :] = sums[part] * pore

    inner(0)
    inner(ROWS - 1)

    @pl.loop(1, ROWS - 1, unroll=2)
    def _(row):
        inner(row)


def carried_kernel(part_ref, mask_ref, xlow_ref, xhigh_ref, out_ref):
    out_ref[...] = part_ref[...]
    for pops, edge, halo in ((X_UP, 0, xlow_ref), (X_DOWN, 7, xhigh_ref)):
        values = [roll_y(halo[k, pl.ds(0, ROWS), :], VEL[i][1]) for k, i in enumerate(pops)]
        pore = mask_ref[column(edge), :].astype(jnp.float32)
        for part in range(3):
            total = None
            for k, i in enumerate(pops):
                sign = VEL[i][part]
                if sign:
                    term = values[k] if sign == 1 else -values[k]
                    total = term if total is None else total + term
            out_ref[part, column(edge), :] = part_ref[part, column(edge), :] + pore * total


def flow_out_kernel(post_ref, below_ref, above_ref, xlow_ref, xhigh_ref, out_ref):
    def inner(row):
        for i in range(19):
            out_ref[i, tile(row), :] = streamed(post_ref, below_ref, above_ref, i, row)

    inner(0)
    inner(ROWS - 1)

    @pl.loop(1, ROWS - 1, unroll=2)
    def _(row):
        inner(row)

    for pops, edge, halo in ((X_UP, 0, xlow_ref), (X_DOWN, 7, xhigh_ref)):
        for k, i in enumerate(pops):
            out_ref[i, column(edge), :] = roll_y(halo[k, pl.ds(0, ROWS), :], VEL[i][1])


def tracer_collide(g, flow):
    total = ((g[0] + g[1]) + (g[2] + g[3])) + ((g[4] + g[5]) + g[6])
    scaled = 0.125 * total
    out = [g[0] - 1.25 * (g[0] - 0.25 * total)]
    for part in range(3):
        lean = 4.0 * flow[part]
        up, down = g[1 + 2 * part], g[2 + 2 * part]
        out.append(up - 1.25 * (up - scaled * (1.0 + lean)))
        out.append(down - 1.25 * (down - scaled * (1.0 - lean)))
    return out


def inside():
    position = lax.axis_index("gz")
    return (position > 0).astype(jnp.int32), (position < lax.axis_size("gz") - 1).astype(jnp.int32)


def tracer_window_kernel(shift_ref, own_ref, next_ref, win_ref, up_ref, down_ref, total_ref):
    shift, (keep_low, _) = shift_ref[0], inside()
    win_ref[:, tile(0), :] = jnp.zeros((7, SIDE, LANES), jnp.float32)
    win_ref[:, tile(35), :] = jnp.zeros((7, SIDE, LANES), jnp.float32)

    @pl.loop(jnp.maximum(-2, -shift), ROWS - shift)
    def _(row):
        keep = (row >= 0) | (keep_low > 0)
        for i in range(7):
            win_ref[i, tile(row + 2), :] = jnp.where(keep, own_ref[i, tile(row + shift), :], 0.0)

    @pl.loop(ROWS - shift, jnp.minimum(ROWS + 2, 2 * ROWS - shift))
    def _(row):
        keep = (row >= 0) | (keep_low > 0)
        for i in range(7):
            win_ref[i, tile(row + 2), :] = jnp.where(keep, next_ref[i, tile(row + shift - ROWS), :], 0.0)

    total_ref[...] = ((win_ref[0] + win_ref[1]) + (win_ref[2] + win_ref[3])) + ((win_ref[4] + win_ref[5]) + win_ref[6])
    for out, near, away, i in ((up_ref, 7, 6, 1), (down_ref, 0, 1, 2)):
        out[...] = jnp.zeros_like(out)
        still = win_ref[0, column(near, ROWS, 2), :]
        across = roll_y(win_ref[3, column(near, ROWS, 2), :], 1) + roll_y(win_ref[4, column(near, ROWS, 2), :], -1)
        along = win_ref[5, column(near, ROWS, 1), :] + win_ref[6, column(near, ROWS, 3), :]
        out[0, pl.ds(0, ROWS), :] = still + across + along
        out[1] = win_ref[i, column(near, 34, 1), :]
        out[2] = total_ref[column(near, 34, 1), :]
        out[3, pl.ds(0, ROWS), :] = win_ref[i, column(away, ROWS, 2), :]
        out[4, pl.ds(0, ROWS), :] = total_ref[column(away, ROWS, 2), :]


def flow_window_kernel(shift_ref, here_ref, beyond_ref, far_ref, out_ref, up_ref, down_ref):
    shift = shift_ref[0]

    @pl.when(shift == 1)
    def _():
        out_ref[:, tile(0), :] = far_ref[0:3]

    @pl.when(shift == ROWS - 1)
    def _():
        out_ref[:, tile(35), :] = far_ref[0:3]

    @pl.loop(jnp.maximum(-2, -shift), ROWS - shift)
    def _(row):
        for part in range(3):
            out_ref[part, tile(row + 2), :] = here_ref[part, tile(row + shift), :]

    @pl.loop(ROWS - shift, jnp.minimum(ROWS + 2, 2 * ROWS - shift))
    def _(row):
        for part in range(3):
            out_ref[part, tile(row + 2), :] = beyond_ref[part, tile(row + shift - ROWS), :]

    for out, near, away in ((up_ref, 7, 6), (down_ref, 0, 1)):
        for part in range(3):
            out[part] = out_ref[part, column(near, 34, 1), :]
        out[3] = out_ref[0, column(away, 34, 1), :]


def tracer_first_kernel(shift_ref, win_ref, far_ref, flow_ref, post_ref):
    shift = shift_ref[0]

    def store(row, g):
        post = tracer_collide(g, [flow_ref[part, tile(row), :] for part in range(3)])
        for i in range(7):
            post_ref[i, tile(row), :] = post[i]

    @pl.loop(0, 36, unroll=2)
    def _(row):
        store(row, [win_ref[i, tile(row), :] for i in range(7)])

    @pl.when(shift == 1)
    def _():
        store(0, [far_ref[3 + i] for i in range(7)])

    @pl.when(shift == ROWS - 1)
    def _():
        store(35, [far_ref[3 + i] for i in range(7)])


def tracer_streamed(post_ref, i, row, low, high):
    if i == 5:
        return post_ref[5, tile(row - 1), :]
    if i == 6:
        return post_ref[6, tile(row + 1), :]
    value = post_ref[i, tile(row), :]
    sub = sublane()
    if i == 1:
        return jnp.where(sub == 0, low, roll_x(value, 1))
    if i == 2:
        return jnp.where(sub == SIDE - 1, high, roll_x(value, -1))
    return roll_y(value, (0, 0, 0, 1, -1)[i])


def beside(post_ref, tracer_ref, flow_ref, sign, own, edge):
    mean = 0.125 * tracer_ref[7]
    lean_x, lean_y, lean_z = (4.0 * flow_ref[part] for part in range(3))
    g = tracer_ref[6]
    near = g - 1.25 * (g - mean * (1.0 + sign * lean_x))
    g, scaled = tracer_ref[8, :ROWS], 0.125 * tracer_ref[9, :ROWS]
    away = g - 1.25 * (g - scaled * (1.0 + sign * 4.0 * flow_ref[3, 1 : 1 + ROWS]))
    inner = slice(1, 1 + ROWS)
    rest = 2.0 * mean[inner] + roll_y(mean[inner] * (1.0 + lean_y[inner]), 1) + roll_y(mean[inner] * (1.0 - lean_y[inner]), -1)
    rest = rest + (mean * (1.0 + lean_z))[:ROWS] + (mean * (1.0 - lean_z))[2:]
    total = 1.25 * rest - 0.25 * tracer_ref[5, :ROWS] + away + post_ref[own, column(edge, ROWS, 2), :]
    return near, away - 1.25 * (away - 0.125 * total * (1.0 + sign * lean_x[inner]))


def tracer_second_kernel(post_ref, xlow_ref, xhigh_ref, flow_low_ref, flow_high_ref, flow_ref, out_ref, next_ref, edge_ref):
    keep_low, keep_high = inside()
    low, low_next = beside(post_ref, xlow_ref, flow_low_ref, 1.0, 2, 0)
    high, high_next = beside(post_ref, xhigh_ref, flow_high_ref, -1.0, 1, 7)
    edge_ref[column(0, 34), :] = low
    edge_ref[column(7, 34), :] = high

    @pl.loop(-1, ROWS + 1, unroll=2)
    def _(row):
        edge = edge_ref[tile(row + 1), :]
        g = [tracer_streamed(post_ref, i, row + 2, edge, edge) for i in range(7)]
        post = tracer_collide(g, [flow_ref[part, tile(row + 2), :] for part in range(3)])
        keep = jnp.where(row < 0, keep_low, jnp.where(row >= ROWS, keep_high, 1)) > 0
        for i in range(7):
            next_ref[i, tile(row + 1), :] = jnp.where(keep, post[i], 0.0)

    @pl.loop(0, ROWS, unroll=4)
    def _(row):
        for i in range(7):
            out_ref[i, tile(row), :] = tracer_streamed(next_ref, i, row + 1, 0.0, 0.0)

    out_ref[1, column(0), :] = low_next
    out_ref[2, column(7), :] = high_next


VMEM = pl.BlockSpec(memory_space=pltpu.VMEM)
SMEM = pl.BlockSpec(memory_space=pltpu.SMEM)
ANY = pl.BlockSpec(memory_space=pl.ANY)
HBM = pl.BlockSpec(memory_space=pltpu.HBM)


def hold(value):
    return pltpu.with_memory_space_constraint(value, pltpu.HBM)


def room(*shape, dtype=jnp.float32):
    return pltpu.VMEM(shape, dtype)


def call(kernel, outs, args, specs=None, scratch=(), out_specs=None, work=None):
    shapes = [jax.ShapeDtypeStruct(s, jnp.float32) for s in outs]
    return pl.pallas_call(
        kernel,
        out_shape=shapes,
        in_specs=specs or [VMEM] * len(args),
        out_specs=out_specs or [VMEM] * len(shapes),
        scratch_shapes=list(scratch),
        compiler_params=PARAMS,
        cost_estimate=work and pl.CostEstimate(flops=work, bytes_accessed=5 * 10**6, transcendentals=0),
    )(*args)


def ring(value, axis, by):
    count = lax.axis_size(axis)
    if by % count == 0:
        return value
    return lax.ppermute(value, axis, [(i, (i + by) % count) for i in range(count)])


def line(value, axis, by):
    count = lax.axis_size(axis)
    pairs = [(i, i + by) for i in range(count) if 0 <= i + by < count]
    return lax.ppermute(value, axis, pairs)


def place(carried, start):
    def branch(slab):
        def run(carried):
            return ring(carried, "gz", -slab), ring(carried, "gz", -slab - 1)

        return run

    return lax.switch(start, [branch(slab) for slab in range(lax.axis_size("gz"))], carried)


def far_rows(here, beyond, tracer, kind):
    first, last = slice(0, SIDE), slice((ROWS - 1) * SIDE, ROWS * SIDE)

    def none(here, beyond, tracer):
        return jnp.zeros((10, SIDE, LANES), jnp.float32)

    def before(here, beyond, tracer):
        return jnp.concatenate([ring(here[:, last], "gz", 1), line(tracer[:, last], "gz", 1)])

    def after(here, beyond, tracer):
        return jnp.concatenate([ring(beyond[:, first], "gz", -1), line(tracer[:, first], "gz", -2)])

    return lax.switch(kind[0], [none, before, after], here, beyond, tracer)


def body(flow_pops, tracer_pops, pore_mask, relax_rates, window_step, start_slab):
    cells = ROWS * SIDE
    flow = flow_pops.reshape(19, cells, LANES)
    tracer = tracer_pops.reshape(7, cells, LANES)
    mask = pore_mask.reshape(cells, LANES)
    count = lax.axis_size("gz")

    face, block = (160, LANES), (19, cells, LANES)
    kind = jnp.where(window_step == 1, 1, jnp.where(window_step == ROWS - 1, 2, 0))
    start = lax.clamp(jnp.int32(0), lax.rem(start_slab[0], jnp.int32(count)), jnp.int32(count - 1))
    flow_held, mask_held = hold(flow), hold(mask)
    z_up, z_down = call(
        faces_kernel,
        [face, face],
        (start.reshape(1), kind, relax_rates, flow_held, mask_held),
        [SMEM, SMEM, SMEM, HBM, HBM],
        [room(2, 19, 2 * SIDE, LANES), room(2, 2 * SIDE, LANES, dtype=jnp.int32), pltpu.SemaphoreType.DMA((4,))],
    )
    z_low, z_high = ring(z_up, "gz", 1), ring(z_down, "gz", -1)
    post1, side1 = call(
        first_kernel,
        [block, (10, ROWS, LANES)],
        (relax_rates, flow_held, mask_held),
        [SMEM, HBM, HBM],
        [room(*block), room(cells, LANES, dtype=jnp.int32), pltpu.SemaphoreType.DMA((1 + CHUNKS,))],
        work=4 * 10**9,
    )
    tracer_next = line(tracer, "gz", -1)
    window, tracer_up, tracer_down = call(
        tracer_window_kernel,
        [(7, 36 * SIDE, LANES), (5, 34, LANES), (5, 34, LANES)],
        (window_step, tracer, tracer_next),
        [SMEM, VMEM, VMEM],
        [room(36 * SIDE, LANES)],
    )
    up, down = call(pack_kernel, [(5, 34, LANES)] * 2, (side1, z_low, z_high))
    x_low, x_high = ring(up, "gx", 1), ring(down, "gx", -1)
    post2, below, above, up, down = call(
        second_kernel,
        [block, (5, SIDE, LANES), (5, SIDE, LANES), (10, 34, LANES), (10, 34, LANES)],
        (relax_rates, post1, mask, z_low, z_high, x_low, x_high, tracer_up, tracer_down),
        [SMEM] + [VMEM] * 8,
        [room(5, 34 * SIDE, LANES)],
    )
    x_low, x_high = ring(up, "gx", 1), ring(down, "gx", -1)
    (partial,) = call(momentum_kernel, [(3, cells, LANES)], (post2, below, above, mask))
    (carried,) = call(carried_kernel, [(3, cells, LANES)], (partial, mask, x_low, x_high))
    (flow_out,) = call(flow_out_kernel, [block], (post2, below, above, x_low, x_high))
    here, beyond = place(carried, start)
    far = far_rows(here, beyond, tracer, kind)
    flow_window, up, down = call(
        flow_window_kernel,
        [(3, 36 * SIDE, LANES), (4, 34, LANES), (4, 34, LANES)],
        (window_step, here, beyond, far),
        [SMEM] + [VMEM] * 3,
    )
    flow_low, flow_high = ring(up, "gx", 1), ring(down, "gx", -1)
    (post3,) = call(
        tracer_first_kernel,
        [(7, 36 * SIDE, LANES)],
        (window_step, window, far, flow_window),
        [SMEM] + [VMEM] * 3,
    )
    (tracer_out,) = call(
        tracer_second_kernel,
        [(7, cells, LANES)],
        (post3, x_low, x_high, flow_low, flow_high, flow_window),
        scratch=[room(7, 34 * SIDE, LANES), room(34 * SIDE, LANES)],
    )
    return flow_out.reshape(flow_pops.shape), tracer_out.reshape(tracer_pops.shape)


def solution(mesh):
    wide = P(None, "gz", "gx", None)
    return jax.shard_map(
        body,
        mesh=mesh,
        in_specs=(wide, wide, P("gz", "gx", None), P(), P(), P()),
        out_specs=(wide, wide),
        check_vma=False,
    )
```

```python
import jax
import jax.numpy as jnp
import numpy as np
from jax import lax
from jax.experimental import pallas as pl
from jax.experimental.pallas import tpu as pltpu
from jax.sharding import PartitionSpec as P

ROWS = 32
SIDE = 8
LANES = 128
CHUNKS = 4
PART = 18
PARAMS = pltpu.CompilerParams(vmem_limit_bytes=12 * 1024 * 1024)

VEL = [
    (0, 0, 0), (1, 0, 0), (-1, 0, 0), (0, 1, 0), (0, -1, 0), (0, 0, 1), (0, 0, -1),
    (1, 1, 0), (-1, -1, 0), (1, -1, 0), (-1, 1, 0), (1, 0, 1), (-1, 0, -1),
    (1, 0, -1), (-1, 0, 1), (0, 1, 1), (0, -1, -1), (0, 1, -1), (0, -1, 1),
]
X_UP = [1, 7, 9, 11, 13]
X_DOWN = [2, 8, 10, 12, 14]
Z_UP = [5, 11, 14, 15, 18]
Z_DOWN = [6, 12, 13, 16, 17]
Z_FLAT = [0, 1, 2, 3, 4, 7, 8, 9, 10]
LOW_PLANE = {(i, 1): n for n, i in enumerate(Z_FLAT + Z_UP)}
LOW_PLANE.update({(i, 2): 14 + n for n, i in enumerate(Z_UP)})
HIGH_PLANE = {(i, 1): n for n, i in enumerate(Z_FLAT + Z_DOWN)}
HIGH_PLANE.update({(i, 2): 14 + n for n, i in enumerate(Z_DOWN)})
PAIRS = [(1, 2), (3, 4), (5, 6), (7, 8), (9, 10), (11, 12), (13, 14), (15, 16), (17, 18)]
NORMS = [19, 2394, 252, 10, 40, 10, 40, 10, 40, 36, 72, 12, 24, 4, 4, 4, 8, 8, 8]


def rates_of(rates_ref):
    return [rates_ref[k] * np.float32(1.0 / NORMS[k]) for k in range(19)]


def collide(f, pore, c):
    e = [f[a] + f[b] for a, b in PAIRS]
    o = [f[a] - f[b] for a, b in PAIRS]
    rho = f[0] + ((e[0] + e[1]) + (e[2] + e[3])) + ((e[4] + e[5]) + (e[6] + e[7]) + e[8])
    jx = o[0] + (o[3] + o[4]) + (o[5] + o[6])
    jy = o[1] + (o[3] - o[4]) + (o[7] + o[8])
    jz = o[2] + (o[5] - o[6]) + (o[7] - o[8])
    xx, yy, zz = jx * jx, jy * jy, jz * jz
    base = rho - 1.5 * (xx + yy + zz)
    axis, diag = base * np.float32(1 / 9), base * np.float32(1 / 18)
    d0 = f[0] - base * np.float32(1 / 3)
    third, sixth = np.float32(1 / 3), np.float32(1 / 6)
    de = [e[0] - (axis + 0.5 * xx), e[1] - (axis + 0.5 * yy), e[2] - (axis + 0.5 * zz)]
    do = [o[0] - third * jx, o[1] - third * jy, o[2] - third * jz]
    for n, p in enumerate((jx + jy, jx - jy, jx + jz, jx - jz, jy + jz, jy - jz)):
        de.append(e[3 + n] - (diag + 0.25 * (p * p)))
        do.append(o[3 + n] - sixth * p)
    a = de[0] + de[1] + de[2]
    pxy, pxz, pyz = de[3] + de[4], de[5] + de[6], de[7] + de[8]
    b = pxy + pxz + pyz
    a9, b9 = 3.0 * de[0] - a, b - 3.0 * pyz
    a11, b11 = de[1] - de[2], pxy - pxz
    sxy, txy = do[3] + do[4], do[3] - do[4]
    sxz, txz = do[5] + do[6], do[5] - do[6]
    syz, tyz = do[7] + do[8], do[7] - do[8]
    restx, resty, restz = sxy + sxz, txy + syz, txz + tyz
    n = [
        c[0] * (d0 + a + b),
        c[1] * (8.0 * b - 11.0 * a - 30.0 * d0),
        c[2] * (12.0 * d0 - 4.0 * a + b),
        c[3] * (do[0] + restx),
        c[4] * (restx - 4.0 * do[0]),
        c[5] * (do[1] + resty),
        c[6] * (resty - 4.0 * do[1]),
        c[7] * (do[2] + restz),
        c[8] * (restz - 4.0 * do[2]),
        c[9] * (a9 + b9),
        c[10] * (b9 - 2.0 * a9),
        c[11] * (a11 + b11),
        c[12] * (b11 - 2.0 * a11),
        c[13] * (de[3] - de[4]),
        c[14] * (de[7] - de[8]),
        c[15] * (de[5] - de[6]),
        c[16] * (sxy - sxz),
        c[17] * (syz - txy),
        c[18] * (txz - tyz),
    ]
    r0 = n[0] - 30.0 * n[1] + 12.0 * n[2]
    ax = n[0] - 11.0 * n[1] - 4.0 * n[2]
    dg = n[0] + 8.0 * n[1] + n[2]
    u, v = n[9] - 2.0 * n[10], n[11] - 2.0 * n[12]
    p, q = n[9] + n[10], n[11] + n[12]
    exy, exz, eyz = dg + p + q, dg + p - q, dg - 2.0 * p
    ev = [ax + 2.0 * u, ax - u + v, ax - u - v, exy + n[13], exy - n[13], exz + n[15], exz - n[15], eyz + n[14], eyz - n[14]]
    gx, gy, gz = n[3] + n[4], n[5] + n[6], n[7] + n[8]
    xa, ya = gx + n[16], gy - n[17]
    xb, zb = gx - n[16], gz + n[18]
    yc, zc = gy + n[17], gz - n[18]
    od = [n[3] - 4.0 * n[4], n[5] - 4.0 * n[6], n[7] - 4.0 * n[8], xa + ya, xa - ya, xb + zb, xb - zb, yc + zc, yc - zc]
    out = [None] * 19
    out[0] = jnp.where(pore, f[0] - r0, f[0])
    for m, (i, k) in enumerate(PAIRS):
        out[i] = jnp.where(pore, f[i] - (ev[m] + od[m]), f[k])
        out[k] = jnp.where(pore, f[k] - (ev[m] - od[m]), f[i])
    return out


def tile(row):
    start = row * SIDE
    if not isinstance(row, int):
        start = pl.multiple_of(start, SIDE)
    return pl.ds(start, SIDE)


def column(side, count=ROWS, first=0):
    return pl.ds(first * SIDE + side, count, stride=SIDE)


def roll_y(value, by):
    return value if by == 0 else pltpu.roll(value, by % LANES, axis=value.ndim - 1)


def roll_x(value, by):
    return value if by == 0 else pltpu.roll(value, by % SIDE, axis=0)


def sublane():
    return lax.broadcasted_iota(jnp.int32, (SIDE, LANES), 0)


def fetch(pairs, sems, first=0):
    copies = [pltpu.make_async_copy(src, dst, sems.at[first + n]) for n, (src, dst) in enumerate(pairs)]
    for copy in copies:
        copy.start()
    return copies


def halves(ref):
    span = ROWS * SIDE // CHUNKS
    parts = [pl.ds(n * span, span) for n in range(CHUNKS)]
    return [ref.at[:, part, :] for part in parts]


def faces_kernel(start_ref, kind_ref, rates_ref, flow_ref, mask_ref, up_ref, down_ref, pops_ref, pore_ref, sems):
    del start_ref, kind_ref
    ends = (pl.ds(0, 2 * SIDE), pl.ds((ROWS - 2) * SIDE, 2 * SIDE))
    pairs = [(flow_ref.at[:, end, :], pops_ref.at[n]) for n, end in enumerate(ends)]
    pairs += [(mask_ref.at[end, :], pore_ref.at[n]) for n, end in enumerate(ends)]
    copies = fetch(pairs, sems)
    c = rates_of(rates_ref)
    for copy in copies:
        copy.wait()
    for end, out, table in ((0, down_ref, HIGH_PLANE), (1, up_ref, LOW_PLANE)):
        for row in range(2):
            near = row == end
            pore = pore_ref[end, tile(row), :]
            post = collide([pops_ref[end, i, tile(row), :] for i in range(19)], pore == 1, c)
            for (i, depth), plane in table.items():
                if (depth == 1) == near:
                    out[tile(plane), :] = post[i]
            if near:
                out[tile(19), :] = pore.astype(jnp.float32)


def first_kernel(rates_ref, flow_ref, mask_ref, post_ref, side_ref, held_ref, pore_ref, sems):
    copies = fetch([(mask_ref, pore_ref)] + list(zip(halves(flow_ref), halves(held_ref))), sems)
    c = rates_of(rates_ref)
    copies[0].wait()
    for n in range(CHUNKS):
        copies[1 + n].wait()

        @pl.loop(n * ROWS // CHUNKS, (n + 1) * ROWS // CHUNKS)
        def _(row):
            post = collide([held_ref[i, tile(row), :] for i in range(19)], pore_ref[tile(row), :] == 1, c)
            for i in range(19):
                post_ref[i, tile(row), :] = post[i]

    for k in range(5):
        side_ref[k] = post_ref[X_UP[k], column(7), :]
        side_ref[5 + k] = post_ref[X_DOWN[k], column(0), :]


def pack_kernel(side_ref, low_ref, high_ref, up_ref, down_ref):
    for base, pops, edge, out in ((0, X_UP, 7, up_ref), (5, X_DOWN, 0, down_ref)):
        for k, i in enumerate(pops):
            cz = VEL[i][2]
            out[k, pl.ds(1 + cz, ROWS), :] = side_ref[base + k]
            for spot in range(1 + cz):
                plane = LOW_PLANE[(i, 1 + cz - spot)]
                out[k, pl.ds(spot, 1), :] = low_ref[pl.ds(plane * SIDE + edge, 1), :]
            for spot in range(33 + cz, 34):
                plane = HIGH_PLANE[(i, spot - 32 - cz)]
                out[k, pl.ds(spot, 1), :] = high_ref[pl.ds(plane * SIDE + edge, 1), :]


def second_kernel(rates_ref, post_ref, mask_ref, low_ref, high_ref, xlow_ref, xhigh_ref,
                  out_ref, below_ref, above_ref, up_ref, down_ref, edge_ref):
    c = rates_of(rates_ref)
    for k in range(5):
        edge_ref[k, column(0, 34), :] = xlow_ref[k]
        edge_ref[k, column(7, 34), :] = xhigh_ref[k]
    sub = sublane()
    first, last = sub == 0, sub == SIDE - 1

    def source(i, row):
        if isinstance(row, int) and row < 0:
            return low_ref[tile(LOW_PLANE[(i, -row)]), :]
        if isinstance(row, int) and row >= ROWS:
            return high_ref[tile(HIGH_PLANE[(i, row - ROWS + 1)]), :]
        return post_ref[i, tile(row), :]

    def step(row, pore):
        f = []
        for i, (cx, cy, cz) in enumerate(VEL):
            value = source(i, row - cz)
            if cx == 1:
                value = jnp.where(first, edge_ref[X_UP.index(i), tile(row + 1), :], roll_x(value, 1))
            if cx == -1:
                value = jnp.where(last, edge_ref[X_DOWN.index(i), tile(row + 1), :], roll_x(value, -1))
            f.append(roll_y(value, cy))
        return collide(f, pore, c)

    def inner(row):
        post = step(row, mask_ref[tile(row), :] == 1)
        for i in range(19):
            out_ref[i, tile(row), :] = post[i]

    post = step(-1, low_ref[tile(19), :] == 1.0)
    for k, i in enumerate(Z_UP):
        below_ref[k] = post[i]
    post = step(ROWS, high_ref[tile(19), :] == 1.0)
    for k, i in enumerate(Z_DOWN):
        above_ref[k] = post[i]
    inner(0)
    inner(ROWS - 1)

    @pl.loop(1, ROWS - 1, unroll=2)
    def _(row):
        inner(row)

    for pops, edge, out in ((X_UP, 7, up_ref), (X_DOWN, 0, down_ref)):
        for k, i in enumerate(pops):
            cz = VEL[i][2]
            value = out_ref[i, column(edge), :]
            if cz == 0:
                out[k, pl.ds(0, ROWS), :] = value
            elif cz == 1:
                out[k, pl.ds(1, ROWS - 1), :] = value[: ROWS - 1]
                out[k, pl.ds(0, 1), :] = below_ref[Z_UP.index(i), pl.ds(edge, 1), :]
            else:
                out[k, pl.ds(0, ROWS - 1), :] = value[1:]
                out[k, pl.ds(ROWS - 1, 1), :] = above_ref[Z_DOWN.index(i), pl.ds(edge, 1), :]


def streamed(post_ref, below_ref, above_ref, i, row):
    cx, cy, cz = VEL[i]
    if isinstance(row, int) and row - cz < 0:
        value = below_ref[Z_UP.index(i)]
    elif isinstance(row, int) and row - cz >= ROWS:
        value = above_ref[Z_DOWN.index(i)]
    else:
        value = post_ref[i, tile(row - cz), :]
    return roll_y(roll_x(value, cx), cy)


def momentum_kernel(post_ref, below_ref, above_ref, mask_ref, out_ref):
    sub = sublane()
    not_first, not_last = sub > 0, sub < SIDE - 1

    def inner(row):
        sums = [None, None, None]
        for i in range(1, 19):
            value = streamed(post_ref, below_ref, above_ref, i, row)
            if VEL[i][0] == 1:
                value = jnp.where(not_first, value, 0.0)
            if VEL[i][0] == -1:
                value = jnp.where(not_last, value, 0.0)
            for part in range(3):
                sign = VEL[i][part]
                if sign == 1:
                    sums[part] = value if sums[part] is None else sums[part] + value
                if sign == -1:
                    sums[part] = sums[part] - value
        pore = mask_ref[tile(row), :].astype(jnp.float32)
        for part in range(3):
            out_ref[part, tile(row), :] = sums[part] * pore

    inner(0)
    inner(ROWS - 1)

    @pl.loop(1, ROWS - 1, unroll=2)
    def _(row):
        inner(row)


def carried_kernel(part_ref, mask_ref, xlow_ref, xhigh_ref, out_ref):
    out_ref[...] = part_ref[...]
    for pops, edge, halo in ((X_UP, 0, xlow_ref), (X_DOWN, 7, xhigh_ref)):
        values = [roll_y(halo[k, pl.ds(0, ROWS), :], VEL[i][1]) for k, i in enumerate(pops)]
        pore = mask_ref[column(edge), :].astype(jnp.float32)
        for part in range(3):
            total = None
            for k, i in enumerate(pops):
                sign = VEL[i][part]
                if sign:
                    term = values[k] if sign == 1 else -values[k]
                    total = term if total is None else total + term
            out_ref[part, column(edge), :] = part_ref[part, column(edge), :] + pore * total


def flow_out_kernel(post_ref, below_ref, above_ref, xlow_ref, xhigh_ref, out_ref):
    def inner(row):
        for i in range(19):
            out_ref[i, tile(row), :] = streamed(post_ref, below_ref, above_ref, i, row)

    inner(0)
    inner(ROWS - 1)

    @pl.loop(1, ROWS - 1, unroll=2)
    def _(row):
        inner(row)

    for pops, edge, halo in ((X_UP, 0, xlow_ref), (X_DOWN, 7, xhigh_ref)):
        for k, i in enumerate(pops):
            out_ref[i, column(edge), :] = roll_y(halo[k, pl.ds(0, ROWS), :], VEL[i][1])


def tracer_collide(g, flow):
    total = ((g[0] + g[1]) + (g[2] + g[3])) + ((g[4] + g[5]) + g[6])
    scaled = 0.125 * total
    out = [g[0] - 1.25 * (g[0] - 0.25 * total)]
    for part in range(3):
        lean = 4.0 * flow[part]
        up, down = g[1 + 2 * part], g[2 + 2 * part]
        out.append(up - 1.25 * (up - scaled * (1.0 + lean)))
        out.append(down - 1.25 * (down - scaled * (1.0 - lean)))
    return out


def inside():
    position = lax.axis_index("gz")
    return (position > 0).astype(jnp.int32), (position < lax.axis_size("gz") - 1).astype(jnp.int32)


def window_kernel(shift_ref, own_ref, next_ref, rest_ref, here_ref, beyond_ref, far_ref,
                  win_ref, flow_ref, up_ref, down_ref, total_ref):
    shift, (keep_low, _) = shift_ref[0], inside()
    blank = jnp.zeros((7, SIDE, LANES), jnp.float32)
    for end, when in ((0, 1), (35, ROWS - 1)):
        win_ref[:, tile(end), :] = blank

        @pl.when(shift == when)
        def _():
            flow_ref[:, tile(end), :] = far_ref[0:3]

    def fill(first, last, ref, ref_first, source, source_first):
        @pl.loop(first, last)
        def _(row):
            keep = (row >= 0) | (keep_low > 0)
            for i in range(7):
                win_ref[i, tile(row + 2), :] = jnp.where(keep, ref[i, tile(row + shift - ref_first), :], 0.0)
            for part in range(3):
                flow_ref[part, tile(row + 2), :] = source[part, tile(row + shift - source_first), :]

    edge, turn, end = ROWS - shift, ROWS + PART - shift, jnp.minimum(ROWS + 2, 2 * ROWS - shift)
    fill(jnp.maximum(-2, -shift), edge, own_ref, 0, here_ref, 0)
    fill(edge, jnp.minimum(turn, end), next_ref, ROWS, beyond_ref, ROWS)
    fill(turn, end, rest_ref, ROWS + PART, beyond_ref, ROWS)

    total_ref[...] = ((win_ref[0] + win_ref[1]) + (win_ref[2] + win_ref[3])) + ((win_ref[4] + win_ref[5]) + win_ref[6])
    for out, near, away, i in ((up_ref, 7, 6, 1), (down_ref, 0, 1, 2)):
        for part in range(3):
            out[part] = flow_ref[part, column(near, 34, 1), :]
        out[3] = flow_ref[0, column(away, 34, 1), :]
        still = win_ref[0, column(near, ROWS, 2), :]
        across = roll_y(win_ref[3, column(near, ROWS, 2), :], 1) + roll_y(win_ref[4, column(near, ROWS, 2), :], -1)
        along = win_ref[5, column(near, ROWS, 1), :] + win_ref[6, column(near, ROWS, 3), :]
        for plane in (4, 7, 8):
            out[plane, pl.ds(ROWS, 2), :] = jnp.zeros((2, LANES), jnp.float32)
        out[4, pl.ds(0, ROWS), :] = still + across + along
        out[5] = win_ref[i, column(near, 34, 1), :]
        out[6] = total_ref[column(near, 34, 1), :]
        out[7, pl.ds(0, ROWS), :] = win_ref[i, column(away, ROWS, 2), :]
        out[8, pl.ds(0, ROWS), :] = total_ref[column(away, ROWS, 2), :]


def tracer_first_kernel(shift_ref, win_ref, far_ref, flow_ref, post_ref):
    shift = shift_ref[0]

    def store(row, g):
        post = tracer_collide(g, [flow_ref[part, tile(row), :] for part in range(3)])
        for i in range(7):
            post_ref[i, tile(row), :] = post[i]

    @pl.loop(0, 36, unroll=2)
    def _(row):
        store(row, [win_ref[i, tile(row), :] for i in range(7)])

    @pl.when(shift == 1)
    def _():
        store(0, [far_ref[3 + i] for i in range(7)])

    @pl.when(shift == ROWS - 1)
    def _():
        store(35, [far_ref[3 + i] for i in range(7)])


def tracer_streamed(post_ref, i, row, low, high):
    if i == 5:
        return post_ref[5, tile(row - 1), :]
    if i == 6:
        return post_ref[6, tile(row + 1), :]
    value = post_ref[i, tile(row), :]
    sub = sublane()
    if i == 1:
        return jnp.where(sub == 0, low, roll_x(value, 1))
    if i == 2:
        return jnp.where(sub == SIDE - 1, high, roll_x(value, -1))
    return roll_y(value, (0, 0, 0, 1, -1)[i])


def beside(post_ref, side_ref, sign, own, edge):
    mean = 0.125 * side_ref[6]
    lean_x, lean_y, lean_z = (4.0 * side_ref[part] for part in range(3))
    g = side_ref[5]
    near = g - 1.25 * (g - mean * (1.0 + sign * lean_x))
    g, scaled = side_ref[7, :ROWS], 0.125 * side_ref[8, :ROWS]
    away = g - 1.25 * (g - scaled * (1.0 + sign * 4.0 * side_ref[3, 1 : 1 + ROWS]))
    inner = slice(1, 1 + ROWS)
    rest = 2.0 * mean[inner] + roll_y(mean[inner] * (1.0 + lean_y[inner]), 1) + roll_y(mean[inner] * (1.0 - lean_y[inner]), -1)
    rest = rest + (mean * (1.0 + lean_z))[:ROWS] + (mean * (1.0 - lean_z))[2:]
    total = 1.25 * rest - 0.25 * side_ref[4, :ROWS] + away + post_ref[own, column(edge, ROWS, 2), :]
    return near, away - 1.25 * (away - 0.125 * total * (1.0 + sign * lean_x[inner]))


def tracer_second_kernel(post_ref, low_ref, high_ref, flow_ref, out_ref, next_ref, edge_ref):
    keep_low, keep_high = inside()
    low, low_next = beside(post_ref, low_ref, 1.0, 2, 0)
    high, high_next = beside(post_ref, high_ref, -1.0, 1, 7)
    edge_ref[column(0, 34), :] = low
    edge_ref[column(7, 34), :] = high

    @pl.loop(-1, ROWS + 1, unroll=2)
    def _(row):
        edge = edge_ref[tile(row + 1), :]
        g = [tracer_streamed(post_ref, i, row + 2, edge, edge) for i in range(7)]
        post = tracer_collide(g, [flow_ref[part, tile(row + 2), :] for part in range(3)])
        keep = jnp.where(row < 0, keep_low, jnp.where(row >= ROWS, keep_high, 1)) > 0
        for i in range(7):
            next_ref[i, tile(row + 1), :] = jnp.where(keep, post[i], 0.0)

    @pl.loop(0, ROWS, unroll=4)
    def _(row):
        for i in range(7):
            out_ref[i, tile(row), :] = tracer_streamed(next_ref, i, row + 1, 0.0, 0.0)

    out_ref[1, column(0), :] = low_next
    out_ref[2, column(7), :] = high_next


VMEM = pl.BlockSpec(memory_space=pltpu.VMEM)
SMEM = pl.BlockSpec(memory_space=pltpu.SMEM)
ANY = pl.BlockSpec(memory_space=pl.ANY)
HBM = pl.BlockSpec(memory_space=pltpu.HBM)


def hold(value):
    return pltpu.with_memory_space_constraint(value, pltpu.HBM)


def room(*shape, dtype=jnp.float32):
    return pltpu.VMEM(shape, dtype)


def call(kernel, outs, args, specs=None, scratch=(), out_specs=None, work=None):
    shapes = [jax.ShapeDtypeStruct(s, jnp.float32) for s in outs]
    return pl.pallas_call(
        kernel,
        out_shape=shapes,
        in_specs=specs or [VMEM] * len(args),
        out_specs=out_specs or [VMEM] * len(shapes),
        scratch_shapes=list(scratch),
        compiler_params=PARAMS,
        cost_estimate=work and pl.CostEstimate(flops=work, bytes_accessed=5 * 10**6, transcendentals=0),
    )(*args)


def ring(value, axis, by):
    count = lax.axis_size(axis)
    if by % count == 0:
        return value
    return lax.ppermute(value, axis, [(i, (i + by) % count) for i in range(count)])


def line(value, axis, by):
    count = lax.axis_size(axis)
    pairs = [(i, i + by) for i in range(count) if 0 <= i + by < count]
    return lax.ppermute(value, axis, pairs)


def place(carried, start):
    def branch(slab):
        def run(carried):
            return ring(carried, "gz", -slab), ring(carried, "gz", -slab - 1)

        return run

    return lax.switch(start, [branch(slab) for slab in range(lax.axis_size("gz"))], carried)


def far_rows(here, beyond, tracer, kind):
    first, last = slice(0, SIDE), slice((ROWS - 1) * SIDE, ROWS * SIDE)

    def none(here, beyond, tracer):
        return jnp.zeros((10, SIDE, LANES), jnp.float32)

    def before(here, beyond, tracer):
        return jnp.concatenate([ring(here[:, last], "gz", 1), line(tracer[:, last], "gz", 1)])

    def after(here, beyond, tracer):
        return jnp.concatenate([ring(beyond[:, first], "gz", -1), line(tracer[:, first], "gz", -2)])

    return lax.switch(kind[0], [none, before, after], here, beyond, tracer)


def body(flow_pops, tracer_pops, pore_mask, relax_rates, window_step, start_slab):
    cells = ROWS * SIDE
    flow = flow_pops.reshape(19, cells, LANES)
    tracer = tracer_pops.reshape(7, cells, LANES)
    mask = pore_mask.reshape(cells, LANES)
    count = lax.axis_size("gz")

    face, block = (160, LANES), (19, cells, LANES)
    kind = jnp.where(window_step == 1, 1, jnp.where(window_step == ROWS - 1, 2, 0))
    start = lax.clamp(jnp.int32(0), lax.rem(start_slab[0], jnp.int32(count)), jnp.int32(count - 1))
    flow_held, mask_held = hold(flow), hold(mask)
    z_up, z_down = call(
        faces_kernel,
        [face, face],
        (start.reshape(1), kind, relax_rates, flow_held, mask_held),
        [SMEM, SMEM, SMEM, HBM, HBM],
        [room(2, 19, 2 * SIDE, LANES), room(2, 2 * SIDE, LANES, dtype=jnp.int32), pltpu.SemaphoreType.DMA((4,))],
    )
    z_low, z_high = ring(z_up, "gz", 1), ring(z_down, "gz", -1)
    post1, side1 = call(
        first_kernel,
        [block, (10, ROWS, LANES)],
        (relax_rates, flow_held, mask_held),
        [SMEM, HBM, HBM],
        [room(*block), room(cells, LANES, dtype=jnp.int32), pltpu.SemaphoreType.DMA((1 + CHUNKS,))],
        work=4 * 10**9,
    )
    tracer_next = line(tracer[:, : PART * SIDE], "gz", -1)
    tracer_rest = line(tracer[:, PART * SIDE :], "gz", -1)
    up, down = call(pack_kernel, [(5, 34, LANES)] * 2, (side1, z_low, z_high))
    x_low, x_high = ring(up, "gx", 1), ring(down, "gx", -1)
    mask_second, tracer_next = lax.optimization_barrier((mask, tracer_next))
    post2, below, above, up, down = call(
        second_kernel,
        [block, (5, SIDE, LANES), (5, SIDE, LANES), (5, ROWS, LANES), (5, ROWS, LANES)],
        (relax_rates, post1, mask_second, z_low, z_high, x_low, x_high),
        [SMEM] + [VMEM] * 6,
        [room(5, 34 * SIDE, LANES)],
    )
    x_low, x_high = ring(up, "gx", 1), ring(down, "gx", -1)
    (partial,) = call(momentum_kernel, [(3, cells, LANES)], (post2, below, above, mask))
    (carried,) = call(carried_kernel, [(3, cells, LANES)], (partial, mask, x_low, x_high))
    (flow_out,) = call(flow_out_kernel, [block], (post2, below, above, x_low, x_high))
    here, beyond = place(carried, start)
    far = far_rows(here, beyond, tracer, kind)
    window, flow_window, up, down = call(
        window_kernel,
        [(7, 36 * SIDE, LANES), (3, 36 * SIDE, LANES), (9, 34, LANES), (9, 34, LANES)],
        (window_step, tracer, tracer_next, tracer_rest, here, beyond, far),
        [SMEM] + [VMEM] * 6,
        [room(36 * SIDE, LANES)],
    )
    low, high = ring(up, "gx", 1), ring(down, "gx", -1)
    (post3,) = call(
        tracer_first_kernel,
        [(7, 36 * SIDE, LANES)],
        (window_step, window, far, flow_window),
        [SMEM] + [VMEM] * 3,
    )
    (tracer_out,) = call(
        tracer_second_kernel,
        [(7, cells, LANES)],
        (post3, low, high, flow_window),
        scratch=[room(7, 34 * SIDE, LANES), room(34 * SIDE, LANES)],
    )
    return flow_out.reshape(flow_pops.shape), tracer_out.reshape(tracer_pops.shape)


def solution(mesh):
    wide = P(None, "gz", "gx", None)
    return jax.shard_map(
        body,
        mesh=mesh,
        in_specs=(wide, wide, P("gz", "gx", None), P(), P(), P()),
        out_specs=(wide, wide),
        check_vma=False,
    )
```

```python
import jax
import jax.numpy as jnp
import numpy as np
from jax import lax
from jax.experimental import pallas as pl
from jax.experimental.pallas import tpu as pltpu
from jax.sharding import PartitionSpec as P

ROWS = 32
SIDE = 8
LANES = 128
CHUNKS = 4
PART = 18
PARAMS = pltpu.CompilerParams(vmem_limit_bytes=12 * 1024 * 1024)

VEL = [
    (0, 0, 0), (1, 0, 0), (-1, 0, 0), (0, 1, 0), (0, -1, 0), (0, 0, 1), (0, 0, -1),
    (1, 1, 0), (-1, -1, 0), (1, -1, 0), (-1, 1, 0), (1, 0, 1), (-1, 0, -1),
    (1, 0, -1), (-1, 0, 1), (0, 1, 1), (0, -1, -1), (0, 1, -1), (0, -1, 1),
]
X_UP = [1, 7, 9, 11, 13]
X_DOWN = [2, 8, 10, 12, 14]
Z_UP = [5, 11, 14, 15, 18]
Z_DOWN = [6, 12, 13, 16, 17]
Z_FLAT = [0, 1, 2, 3, 4, 7, 8, 9, 10]
LOW_PLANE = {(i, 1): n for n, i in enumerate(Z_FLAT + Z_UP)}
LOW_PLANE.update({(i, 2): 14 + n for n, i in enumerate(Z_UP)})
HIGH_PLANE = {(i, 1): n for n, i in enumerate(Z_FLAT + Z_DOWN)}
HIGH_PLANE.update({(i, 2): 14 + n for n, i in enumerate(Z_DOWN)})
PAIRS = [(1, 2), (3, 4), (5, 6), (7, 8), (9, 10), (11, 12), (13, 14), (15, 16), (17, 18)]
NORMS = [19, 2394, 252, 10, 40, 10, 40, 10, 40, 36, 72, 12, 24, 4, 4, 4, 8, 8, 8]


def rates_of(rates_ref):
    return [rates_ref[k] * np.float32(1.0 / NORMS[k]) for k in range(19)]


def collide(f, pore, c):
    e = [f[a] + f[b] for a, b in PAIRS]
    o = [f[a] - f[b] for a, b in PAIRS]
    rho = f[0] + ((e[0] + e[1]) + (e[2] + e[3])) + ((e[4] + e[5]) + (e[6] + e[7]) + e[8])
    jx = o[0] + (o[3] + o[4]) + (o[5] + o[6])
    jy = o[1] + (o[3] - o[4]) + (o[7] + o[8])
    jz = o[2] + (o[5] - o[6]) + (o[7] - o[8])
    xx, yy, zz = jx * jx, jy * jy, jz * jz
    base = rho - 1.5 * (xx + yy + zz)
    axis, diag = base * np.float32(1 / 9), base * np.float32(1 / 18)
    d0 = f[0] - base * np.float32(1 / 3)
    third, sixth = np.float32(1 / 3), np.float32(1 / 6)
    de = [e[0] - (axis + 0.5 * xx), e[1] - (axis + 0.5 * yy), e[2] - (axis + 0.5 * zz)]
    do = [o[0] - third * jx, o[1] - third * jy, o[2] - third * jz]
    for n, p in enumerate((jx + jy, jx - jy, jx + jz, jx - jz, jy + jz, jy - jz)):
        de.append(e[3 + n] - (diag + 0.25 * (p * p)))
        do.append(o[3 + n] - sixth * p)
    a = de[0] + de[1] + de[2]
    pxy, pxz, pyz = de[3] + de[4], de[5] + de[6], de[7] + de[8]
    b = pxy + pxz + pyz
    a9, b9 = 3.0 * de[0] - a, b - 3.0 * pyz
    a11, b11 = de[1] - de[2], pxy - pxz
    sxy, txy = do[3] + do[4], do[3] - do[4]
    sxz, txz = do[5] + do[6], do[5] - do[6]
    syz, tyz = do[7] + do[8], do[7] - do[8]
    restx, resty, restz = sxy + sxz, txy + syz, txz + tyz
    n = [
        c[0] * (d0 + a + b),
        c[1] * (8.0 * b - 11.0 * a - 30.0 * d0),
        c[2] * (12.0 * d0 - 4.0 * a + b),
        c[3] * (do[0] + restx),
        c[4] * (restx - 4.0 * do[0]),
        c[5] * (do[1] + resty),
        c[6] * (resty - 4.0 * do[1]),
        c[7] * (do[2] + restz),
        c[8] * (restz - 4.0 * do[2]),
        c[9] * (a9 + b9),
        c[10] * (b9 - 2.0 * a9),
        c[11] * (a11 + b11),
        c[12] * (b11 - 2.0 * a11),
        c[13] * (de[3] - de[4]),
        c[14] * (de[7] - de[8]),
        c[15] * (de[5] - de[6]),
        c[16] * (sxy - sxz),
        c[17] * (syz - txy),
        c[18] * (txz - tyz),
    ]
    r0 = n[0] - 30.0 * n[1] + 12.0 * n[2]
    ax = n[0] - 11.0 * n[1] - 4.0 * n[2]
    dg = n[0] + 8.0 * n[1] + n[2]
    u, v = n[9] - 2.0 * n[10], n[11] - 2.0 * n[12]
    p, q = n[9] + n[10], n[11] + n[12]
    exy, exz, eyz = dg + p + q, dg + p - q, dg - 2.0 * p
    ev = [ax + 2.0 * u, ax - u + v, ax - u - v, exy + n[13], exy - n[13], exz + n[15], exz - n[15], eyz + n[14], eyz - n[14]]
    gx, gy, gz = n[3] + n[4], n[5] + n[6], n[7] + n[8]
    xa, ya = gx + n[16], gy - n[17]
    xb, zb = gx - n[16], gz + n[18]
    yc, zc = gy + n[17], gz - n[18]
    od = [n[3] - 4.0 * n[4], n[5] - 4.0 * n[6], n[7] - 4.0 * n[8], xa + ya, xa - ya, xb + zb, xb - zb, yc + zc, yc - zc]
    out = [None] * 19
    out[0] = jnp.where(pore, f[0] - r0, f[0])
    for m, (i, k) in enumerate(PAIRS):
        out[i] = jnp.where(pore, f[i] - (ev[m] + od[m]), f[k])
        out[k] = jnp.where(pore, f[k] - (ev[m] - od[m]), f[i])
    return out


def tile(row):
    start = row * SIDE
    if not isinstance(row, int):
        start = pl.multiple_of(start, SIDE)
    return pl.ds(start, SIDE)


def column(side, count=ROWS, first=0):
    return pl.ds(first * SIDE + side, count, stride=SIDE)


def roll_y(value, by):
    return value if by == 0 else pltpu.roll(value, by % LANES, axis=value.ndim - 1)


def roll_x(value, by):
    return value if by == 0 else pltpu.roll(value, by % SIDE, axis=0)


def sublane():
    return lax.broadcasted_iota(jnp.int32, (SIDE, LANES), 0)


def fetch(pairs, sems, first=0):
    copies = [pltpu.make_async_copy(src, dst, sems.at[first + n]) for n, (src, dst) in enumerate(pairs)]
    for copy in copies:
        copy.start()
    return copies


def halves(ref):
    span = ROWS * SIDE // CHUNKS
    parts = [pl.ds(n * span, span) for n in range(CHUNKS)]
    return [ref.at[:, part, :] for part in parts]


def split_kernel(tracer_ref, first_ref, rest_ref, sems):
    cut, rows = PART * SIDE, ROWS * SIDE
    pairs = [(tracer_ref.at[:, pl.ds(0, cut), :], first_ref), (tracer_ref.at[:, pl.ds(cut, rows - cut), :], rest_ref)]
    for copy in fetch(pairs, sems):
        copy.wait()


def faces_kernel(start_ref, kind_ref, rates_ref, flow_ref, mask_ref, up_ref, down_ref, pops_ref, pore_ref, sems):
    del start_ref, kind_ref
    ends = (pl.ds(0, 2 * SIDE), pl.ds((ROWS - 2) * SIDE, 2 * SIDE))
    pairs = [(flow_ref.at[:, end, :], pops_ref.at[n]) for n, end in enumerate(ends)]
    pairs += [(mask_ref.at[end, :], pore_ref.at[n]) for n, end in enumerate(ends)]
    copies = fetch(pairs, sems)
    c = rates_of(rates_ref)
    for copy in copies:
        copy.wait()
    for end, out, table in ((0, down_ref, HIGH_PLANE), (1, up_ref, LOW_PLANE)):
        for row in range(2):
            near = row == end
            pore = pore_ref[end, tile(row), :]
            post = collide([pops_ref[end, i, tile(row), :] for i in range(19)], pore == 1, c)
            for (i, depth), plane in table.items():
                if (depth == 1) == near:
                    out[tile(plane), :] = post[i]
            if near:
                out[tile(19), :] = pore.astype(jnp.float32)


def first_kernel(rates_ref, flow_ref, mask_ref, post_ref, side_ref, held_ref, pore_ref, sems):
    copies = fetch([(mask_ref, pore_ref)] + list(zip(halves(flow_ref), halves(held_ref))), sems)
    c = rates_of(rates_ref)
    copies[0].wait()
    for n in range(CHUNKS):
        copies[1 + n].wait()

        @pl.loop(n * ROWS // CHUNKS, (n + 1) * ROWS // CHUNKS)
        def _(row):
            post = collide([held_ref[i, tile(row), :] for i in range(19)], pore_ref[tile(row), :] == 1, c)
            for i in range(19):
                post_ref[i, tile(row), :] = post[i]

    for k in range(5):
        side_ref[k] = post_ref[X_UP[k], column(7), :]
        side_ref[5 + k] = post_ref[X_DOWN[k], column(0), :]


def pack_kernel(side_ref, low_ref, high_ref, up_ref, down_ref):
    for base, pops, edge, out in ((0, X_UP, 7, up_ref), (5, X_DOWN, 0, down_ref)):
        for k, i in enumerate(pops):
            cz = VEL[i][2]
            out[k, pl.ds(1 + cz, ROWS), :] = side_ref[base + k]
            for spot in range(1 + cz):
                plane = LOW_PLANE[(i, 1 + cz - spot)]
                out[k, pl.ds(spot, 1), :] = low_ref[pl.ds(plane * SIDE + edge, 1), :]
            for spot in range(33 + cz, 34):
                plane = HIGH_PLANE[(i, spot - 32 - cz)]
                out[k, pl.ds(spot, 1), :] = high_ref[pl.ds(plane * SIDE + edge, 1), :]


def second_kernel(rates_ref, post_ref, mask_ref, low_ref, high_ref, xlow_ref, xhigh_ref,
                  out_ref, below_ref, above_ref, up_ref, down_ref, edge_ref):
    c = rates_of(rates_ref)
    for k in range(5):
        edge_ref[k, column(0, 34), :] = xlow_ref[k]
        edge_ref[k, column(7, 34), :] = xhigh_ref[k]
    sub = sublane()
    first, last = sub == 0, sub == SIDE - 1

    def source(i, row):
        if isinstance(row, int) and row < 0:
            return low_ref[tile(LOW_PLANE[(i, -row)]), :]
        if isinstance(row, int) and row >= ROWS:
            return high_ref[tile(HIGH_PLANE[(i, row - ROWS + 1)]), :]
        return post_ref[i, tile(row), :]

    def step(row, pore):
        f = []
        for i, (cx, cy, cz) in enumerate(VEL):
            value = source(i, row - cz)
            if cx == 1:
                value = jnp.where(first, edge_ref[X_UP.index(i), tile(row + 1), :], roll_x(value, 1))
            if cx == -1:
                value = jnp.where(last, edge_ref[X_DOWN.index(i), tile(row + 1), :], roll_x(value, -1))
            f.append(roll_y(value, cy))
        return collide(f, pore, c)

    def inner(row):
        post = step(row, mask_ref[tile(row), :] == 1)
        for i in range(19):
            out_ref[i, tile(row), :] = post[i]

    post = step(-1, low_ref[tile(19), :] == 1.0)
    for k, i in enumerate(Z_UP):
        below_ref[k] = post[i]
    post = step(ROWS, high_ref[tile(19), :] == 1.0)
    for k, i in enumerate(Z_DOWN):
        above_ref[k] = post[i]
    inner(0)
    inner(ROWS - 1)

    @pl.loop(1, ROWS - 1, unroll=2)
    def _(row):
        inner(row)

    for pops, edge, out in ((X_UP, 7, up_ref), (X_DOWN, 0, down_ref)):
        for k, i in enumerate(pops):
            cz = VEL[i][2]
            value = out_ref[i, column(edge), :]
            if cz == 0:
                out[k, pl.ds(0, ROWS), :] = value
            elif cz == 1:
                out[k, pl.ds(1, ROWS - 1), :] = value[: ROWS - 1]
                out[k, pl.ds(0, 1), :] = below_ref[Z_UP.index(i), pl.ds(edge, 1), :]
            else:
                out[k, pl.ds(0, ROWS - 1), :] = value[1:]
                out[k, pl.ds(ROWS - 1, 1), :] = above_ref[Z_DOWN.index(i), pl.ds(edge, 1), :]


def streamed(post_ref, below_ref, above_ref, i, row):
    cx, cy, cz = VEL[i]
    if isinstance(row, int) and row - cz < 0:
        value = below_ref[Z_UP.index(i)]
    elif isinstance(row, int) and row - cz >= ROWS:
        value = above_ref[Z_DOWN.index(i)]
    else:
        value = post_ref[i, tile(row - cz), :]
    return roll_y(roll_x(value, cx), cy)


def momentum_kernel(post_ref, below_ref, above_ref, mask_ref, out_ref):
    sub = sublane()
    not_first, not_last = sub > 0, sub < SIDE - 1

    def inner(row):
        sums = [None, None, None]
        for i in range(1, 19):
            value = streamed(post_ref, below_ref, above_ref, i, row)
            if VEL[i][0] == 1:
                value = jnp.where(not_first, value, 0.0)
            if VEL[i][0] == -1:
                value = jnp.where(not_last, value, 0.0)
            for part in range(3):
                sign = VEL[i][part]
                if sign == 1:
                    sums[part] = value if sums[part] is None else sums[part] + value
                if sign == -1:
                    sums[part] = sums[part] - value
        pore = mask_ref[tile(row), :].astype(jnp.float32)
        for part in range(3):
            out_ref[part, tile(row), :] = sums[part] * pore

    inner(0)
    inner(ROWS - 1)

    @pl.loop(1, ROWS - 1, unroll=2)
    def _(row):
        inner(row)


def carried_kernel(part_ref, mask_ref, xlow_ref, xhigh_ref, out_ref):
    out_ref[...] = part_ref[...]
    for pops, edge, halo in ((X_UP, 0, xlow_ref), (X_DOWN, 7, xhigh_ref)):
        values = [roll_y(halo[k, pl.ds(0, ROWS), :], VEL[i][1]) for k, i in enumerate(pops)]
        pore = mask_ref[column(edge), :].astype(jnp.float32)
        for part in range(3):
            total = None
            for k, i in enumerate(pops):
                sign = VEL[i][part]
                if sign:
                    term = values[k] if sign == 1 else -values[k]
                    total = term if total is None else total + term
            out_ref[part, column(edge), :] = part_ref[part, column(edge), :] + pore * total


def flow_out_kernel(post_ref, below_ref, above_ref, xlow_ref, xhigh_ref, out_ref):
    def inner(row):
        for i in range(19):
            out_ref[i, tile(row), :] = streamed(post_ref, below_ref, above_ref, i, row)

    inner(0)
    inner(ROWS - 1)

    @pl.loop(1, ROWS - 1, unroll=2)
    def _(row):
        inner(row)

    for pops, edge, halo in ((X_UP, 0, xlow_ref), (X_DOWN, 7, xhigh_ref)):
        for k, i in enumerate(pops):
            out_ref[i, column(edge), :] = roll_y(halo[k, pl.ds(0, ROWS), :], VEL[i][1])


def tracer_collide(g, flow):
    total = ((g[0] + g[1]) + (g[2] + g[3])) + ((g[4] + g[5]) + g[6])
    scaled = 0.125 * total
    out = [g[0] - 1.25 * (g[0] - 0.25 * total)]
    for part in range(3):
        lean = 4.0 * flow[part]
        up, down = g[1 + 2 * part], g[2 + 2 * part]
        out.append(up - 1.25 * (up - scaled * (1.0 + lean)))
        out.append(down - 1.25 * (down - scaled * (1.0 - lean)))
    return out


def inside():
    position = lax.axis_index("gz")
    return (position > 0).astype(jnp.int32), (position < lax.axis_size("gz") - 1).astype(jnp.int32)


def window_kernel(shift_ref, own_ref, next_ref, rest_ref, here_ref, beyond_ref, far_ref,
                  win_ref, flow_ref, up_ref, down_ref, total_ref):
    shift, (keep_low, _) = shift_ref[0], inside()
    blank = jnp.zeros((7, SIDE, LANES), jnp.float32)
    for end, when in ((0, 1), (35, ROWS - 1)):
        win_ref[:, tile(end), :] = blank

        @pl.when(shift == when)
        def _():
            flow_ref[:, tile(end), :] = far_ref[0:3]

    def fill(first, last, ref, ref_first, source, source_first):
        @pl.loop(first, last)
        def _(row):
            keep = (row >= 0) | (keep_low > 0)
            for i in range(7):
                win_ref[i, tile(row + 2), :] = jnp.where(keep, ref[i, tile(row + shift - ref_first), :], 0.0)
            for part in range(3):
                flow_ref[part, tile(row + 2), :] = source[part, tile(row + shift - source_first), :]

    edge, turn, end = ROWS - shift, ROWS + PART - shift, jnp.minimum(ROWS + 2, 2 * ROWS - shift)
    fill(jnp.maximum(-2, -shift), edge, own_ref, 0, here_ref, 0)
    fill(edge, jnp.minimum(turn, end), next_ref, ROWS, beyond_ref, ROWS)
    fill(turn, end, rest_ref, ROWS + PART, beyond_ref, ROWS)

    total_ref[...] = ((win_ref[0] + win_ref[1]) + (win_ref[2] + win_ref[3])) + ((win_ref[4] + win_ref[5]) + win_ref[6])
    for out, near, away, i in ((up_ref, 7, 6, 1), (down_ref, 0, 1, 2)):
        for part in range(3):
            out[part] = flow_ref[part, column(near, 34, 1), :]
        out[3] = flow_ref[0, column(away, 34, 1), :]
        still = win_ref[0, column(near, ROWS, 2), :]
        across = roll_y(win_ref[3, column(near, ROWS, 2), :], 1) + roll_y(win_ref[4, column(near, ROWS, 2), :], -1)
        along = win_ref[5, column(near, ROWS, 1), :] + win_ref[6, column(near, ROWS, 3), :]
        for plane in (4, 7, 8):
            out[plane, pl.ds(ROWS, 2), :] = jnp.zeros((2, LANES), jnp.float32)
        out[4, pl.ds(0, ROWS), :] = still + across + along
        out[5] = win_ref[i, column(near, 34, 1), :]
        out[6] = total_ref[column(near, 34, 1), :]
        out[7, pl.ds(0, ROWS), :] = win_ref[i, column(away, ROWS, 2), :]
        out[8, pl.ds(0, ROWS), :] = total_ref[column(away, ROWS, 2), :]


def tracer_first_kernel(shift_ref, win_ref, far_ref, flow_ref, post_ref):
    shift = shift_ref[0]

    def store(row, g):
        post = tracer_collide(g, [flow_ref[part, tile(row), :] for part in range(3)])
        for i in range(7):
            post_ref[i, tile(row), :] = post[i]

    @pl.loop(0, 36, unroll=2)
    def _(row):
        store(row, [win_ref[i, tile(row), :] for i in range(7)])

    @pl.when(shift == 1)
    def _():
        store(0, [far_ref[3 + i] for i in range(7)])

    @pl.when(shift == ROWS - 1)
    def _():
        store(35, [far_ref[3 + i] for i in range(7)])


def tracer_streamed(post_ref, i, row, low, high):
    if i == 5:
        return post_ref[5, tile(row - 1), :]
    if i == 6:
        return post_ref[6, tile(row + 1), :]
    value = post_ref[i, tile(row), :]
    sub = sublane()
    if i == 1:
        return jnp.where(sub == 0, low, roll_x(value, 1))
    if i == 2:
        return jnp.where(sub == SIDE - 1, high, roll_x(value, -1))
    return roll_y(value, (0, 0, 0, 1, -1)[i])


def beside(post_ref, side_ref, sign, own, edge):
    mean = 0.125 * side_ref[6]
    lean_x, lean_y, lean_z = (4.0 * side_ref[part] for part in range(3))
    g = side_ref[5]
    near = g - 1.25 * (g - mean * (1.0 + sign * lean_x))
    g, scaled = side_ref[7, :ROWS], 0.125 * side_ref[8, :ROWS]
    away = g - 1.25 * (g - scaled * (1.0 + sign * 4.0 * side_ref[3, 1 : 1 + ROWS]))
    inner = slice(1, 1 + ROWS)
    rest = 2.0 * mean[inner] + roll_y(mean[inner] * (1.0 + lean_y[inner]), 1) + roll_y(mean[inner] * (1.0 - lean_y[inner]), -1)
    rest = rest + (mean * (1.0 + lean_z))[:ROWS] + (mean * (1.0 - lean_z))[2:]
    total = 1.25 * rest - 0.25 * side_ref[4, :ROWS] + away + post_ref[own, column(edge, ROWS, 2), :]
    return near, away - 1.25 * (away - 0.125 * total * (1.0 + sign * lean_x[inner]))


def tracer_second_kernel(post_ref, low_ref, high_ref, flow_ref, out_ref, next_ref, edge_ref):
    keep_low, keep_high = inside()
    low, low_next = beside(post_ref, low_ref, 1.0, 2, 0)
    high, high_next = beside(post_ref, high_ref, -1.0, 1, 7)
    edge_ref[column(0, 34), :] = low
    edge_ref[column(7, 34), :] = high

    @pl.loop(-1, ROWS + 1, unroll=2)
    def _(row):
        edge = edge_ref[tile(row + 1), :]
        g = [tracer_streamed(post_ref, i, row + 2, edge, edge) for i in range(7)]
        post = tracer_collide(g, [flow_ref[part, tile(row + 2), :] for part in range(3)])
        keep = jnp.where(row < 0, keep_low, jnp.where(row >= ROWS, keep_high, 1)) > 0
        for i in range(7):
            next_ref[i, tile(row + 1), :] = jnp.where(keep, post[i], 0.0)

    @pl.loop(0, ROWS, unroll=4)
    def _(row):
        for i in range(7):
            out_ref[i, tile(row), :] = tracer_streamed(next_ref, i, row + 1, 0.0, 0.0)

    out_ref[1, column(0), :] = low_next
    out_ref[2, column(7), :] = high_next


VMEM = pl.BlockSpec(memory_space=pltpu.VMEM)
SMEM = pl.BlockSpec(memory_space=pltpu.SMEM)
ANY = pl.BlockSpec(memory_space=pl.ANY)
HBM = pl.BlockSpec(memory_space=pltpu.HBM)


def hold(value):
    return pltpu.with_memory_space_constraint(value, pltpu.HBM)


def room(*shape, dtype=jnp.float32):
    return pltpu.VMEM(shape, dtype)


def call(kernel, outs, args, specs=None, scratch=(), out_specs=None, work=None):
    shapes = [jax.ShapeDtypeStruct(s, jnp.float32) for s in outs]
    return pl.pallas_call(
        kernel,
        out_shape=shapes,
        in_specs=specs or [VMEM] * len(args),
        out_specs=out_specs or [VMEM] * len(shapes),
        scratch_shapes=list(scratch),
        compiler_params=PARAMS,
        cost_estimate=work and pl.CostEstimate(flops=work, bytes_accessed=5 * 10**6, transcendentals=0),
    )(*args)


def ring(value, axis, by):
    count = lax.axis_size(axis)
    if by % count == 0:
        return value
    return lax.ppermute(value, axis, [(i, (i + by) % count) for i in range(count)])


def line(value, axis, by):
    count = lax.axis_size(axis)
    pairs = [(i, i + by) for i in range(count) if 0 <= i + by < count]
    return lax.ppermute(value, axis, pairs)


def place(carried, start):
    def branch(slab):
        def run(carried):
            return ring(carried, "gz", -slab), ring(carried, "gz", -slab - 1)

        return run

    return lax.switch(start, [branch(slab) for slab in range(lax.axis_size("gz"))], carried)


def far_rows(here, beyond, tracer, kind):
    first, last = slice(0, SIDE), slice((ROWS - 1) * SIDE, ROWS * SIDE)

    def none(here, beyond, tracer):
        return jnp.zeros((10, SIDE, LANES), jnp.float32)

    def before(here, beyond, tracer):
        return jnp.concatenate([ring(here[:, last], "gz", 1), line(tracer[:, last], "gz", 1)])

    def after(here, beyond, tracer):
        return jnp.concatenate([ring(beyond[:, first], "gz", -1), line(tracer[:, first], "gz", -2)])

    return lax.switch(kind[0], [none, before, after], here, beyond, tracer)


def body(flow_pops, tracer_pops, pore_mask, relax_rates, window_step, start_slab):
    cells = ROWS * SIDE
    flow = flow_pops.reshape(19, cells, LANES)
    tracer = tracer_pops.reshape(7, cells, LANES)
    mask = pore_mask.reshape(cells, LANES)
    count = lax.axis_size("gz")

    face, block = (160, LANES), (19, cells, LANES)
    kind = jnp.where(window_step == 1, 1, jnp.where(window_step == ROWS - 1, 2, 0))
    start = lax.clamp(jnp.int32(0), lax.rem(start_slab[0], jnp.int32(count)), jnp.int32(count - 1))
    flow_held, mask_held = hold(flow), hold(mask)
    z_up, z_down = call(
        faces_kernel,
        [face, face],
        (start.reshape(1), kind, relax_rates, flow_held, mask_held),
        [SMEM, SMEM, SMEM, HBM, HBM],
        [room(2, 19, 2 * SIDE, LANES), room(2, 2 * SIDE, LANES, dtype=jnp.int32), pltpu.SemaphoreType.DMA((4,))],
    )
    z_low, z_high = ring(z_up, "gz", 1), ring(z_down, "gz", -1)
    post1, side1 = call(
        first_kernel,
        [block, (10, ROWS, LANES)],
        (relax_rates, flow_held, mask_held),
        [SMEM, HBM, HBM],
        [room(*block), room(cells, LANES, dtype=jnp.int32), pltpu.SemaphoreType.DMA((1 + CHUNKS,))],
        work=4 * 10**9,
    )
    cut = PART * SIDE
    first, rest = call(
        split_kernel,
        [(7, cut, LANES), (7, cells - cut, LANES)],
        (hold(tracer),),
        [HBM],
        [pltpu.SemaphoreType.DMA((2,))],
    )
    tracer_next, tracer_rest = line(first, "gz", -1), line(rest, "gz", -1)
    up, down = call(pack_kernel, [(5, 34, LANES)] * 2, (side1, z_low, z_high))
    x_low, x_high = ring(up, "gx", 1), ring(down, "gx", -1)
    mask_second, tracer_next = lax.optimization_barrier((mask, tracer_next))
    post2, below, above, up, down = call(
        second_kernel,
        [block, (5, SIDE, LANES), (5, SIDE, LANES), (5, ROWS, LANES), (5, ROWS, LANES)],
        (relax_rates, post1, mask_second, z_low, z_high, x_low, x_high),
        [SMEM] + [VMEM] * 6,
        [room(5, 34 * SIDE, LANES)],
    )
    x_low, x_high = ring(up, "gx", 1), ring(down, "gx", -1)
    (partial,) = call(momentum_kernel, [(3, cells, LANES)], (post2, below, above, mask))
    (carried,) = call(carried_kernel, [(3, cells, LANES)], (partial, mask, x_low, x_high))
    (flow_out,) = call(flow_out_kernel, [block], (post2, below, above, x_low, x_high))
    here, beyond = place(carried, start)
    far = far_rows(here, beyond, tracer, kind)
    window, flow_window, up, down = call(
        window_kernel,
        [(7, 36 * SIDE, LANES), (3, 36 * SIDE, LANES), (9, 34, LANES), (9, 34, LANES)],
        (window_step, tracer, tracer_next, tracer_rest, here, beyond, far),
        [SMEM] + [VMEM] * 6,
        [room(36 * SIDE, LANES)],
    )
    low, high = ring(up, "gx", 1), ring(down, "gx", -1)
    (post3,) = call(
        tracer_first_kernel,
        [(7, 36 * SIDE, LANES)],
        (window_step, window, far, flow_window),
        [SMEM] + [VMEM] * 3,
    )
    (tracer_out,) = call(
        tracer_second_kernel,
        [(7, cells, LANES)],
        (post3, low, high, flow_window),
        scratch=[room(7, 34 * SIDE, LANES), room(34 * SIDE, LANES)],
    )
    return flow_out.reshape(flow_pops.shape), tracer_out.reshape(tracer_pops.shape)


def solution(mesh):
    wide = P(None, "gz", "gx", None)
    return jax.shard_map(
        body,
        mesh=mesh,
        in_specs=(wide, wide, P("gz", "gx", None), P(), P(), P()),
        out_specs=(wide, wide),
        check_vma=False,
    )
```
